32 devices in a mesh: gx: 4 (over y, core), gy: 8 (over z, x).
Axes of the slice: x: 2, y: 2, z: 4, core: 2. Of those that a mesh axis runs over, the one named last changes fastest.
Arguments:
- right_side: float32 [256, 256, 512], P('gx', 'gy'), may hold values from -120 to 120
- diagonal: float32 [256, 256, 512], P('gx', 'gy'), may hold values from 0.002 to 0.2
Outputs:
- update: float32 [256, 256, 512], P('gx', 'gy')
- residual: float32 [256, 256, 512], P('gx', 'gy')
The draws below stay inside these ranges and needn't reach their ends.
All inputs are finite; a program needn't handle non-finite values.
Results may differ from the reference program's by a relative error of at most 0.00028.
Values sent between devices are 32-bit elements; how exact they have to be, the bound alone decides.
A program may use at most 128 MiB of HBM per device.

```python
import math
import jax
import jax.numpy as jnp
from jax import lax

CZ = 512
NX = 256
NY = 256


def draw_right_side(key, part):
    noise = jnp.clip(jax.random.normal(key, (NX, NY, CZ), jnp.float32), -6.0, 6.0)
    along_x = jnp.arange(NX, dtype=jnp.float32) / NX
    along_y = jnp.arange(NY, dtype=jnp.float32) / NY
    scale = (1.0 + 0.75 * along_x)[:, None, None] * (1.0 + 0.75 * along_y)[None, :, None]
    return noise * scale


def level_of(own_key, shape, pieces, smallest, top_value):
    level, own = 1.0, jax.random.fold_in(own_key, 6)
    for position, parts in pieces:
        heights = jnp.exp(jax.random.uniform(jax.random.fold_in(own, position), (parts,), jnp.float32, smallest / len(pieces), top_value / len(pieces)))
        level = level * jnp.repeat(heights, shape[position] // parts).reshape([-1 if axis == position else 1 for axis in range(len(shape))])
    return level


def setup_inputs(seed: int = 0) -> dict:
    key_list = jax.random.split(jax.random.key(seed), 3)
    return {
        "right_side": draw_right_side(jax.random.fold_in(key_list[2], 71), 0),
        "diagonal": jnp.clip(jnp.exp(math.log(0.2) - 4.6051702 * jax.random.uniform(key_list[1], (NX, NY, CZ), jnp.float32) ** level_of(key_list[1], (NX, NY, CZ), ((0, 4), (1, 8)), -0.2, 0.2)), 0.002, 0.2),
    }


relax_weight = 0.8
coarse_sweeps = 8


def neighbour_sum(padded):
    total = padded[2:, 1:-1, 1:-1] + padded[:-2, 1:-1, 1:-1]
    total = total + padded[1:-1, 2:, 1:-1] + padded[1:-1, :-2, 1:-1]
    return total + padded[1:-1, 1:-1, 2:] + padded[1:-1, 1:-1, :-2]


def level_operator(field, padded, coefficient, level):
    return (6.0 * field - neighbour_sum(padded)) * (0.25 ** level) + coefficient * field


def zero_pad(field):
    return jnp.pad(field, 1)


def pair_table(depth):
    fine_index = jnp.arange(depth, dtype=jnp.int32)[:, None] // 2
    coarse_index = jnp.arange(depth // 2, dtype=jnp.int32)[None, :]
    return jnp.where(fine_index == coarse_index, 1.0, 0.0).astype(jnp.float32)


def restrict(field):
    first, second, third = field.shape
    halved = jnp.dot(field.reshape(first * second, third), 0.5 * pair_table(third), precision=lax.Precision.HIGHEST)
    halved = halved.reshape(first // 2, 2, second // 2, 2, third // 2)
    return halved.sum(axis=(1, 3)) * 0.25


def prolong(field):
    first, second, third = field.shape
    doubled = jnp.dot(field.reshape(first * second, third), pair_table(2 * third).T, precision=lax.Precision.HIGHEST)
    doubled = doubled.reshape(first, 1, second, 1, 2 * third)
    doubled = jnp.broadcast_to(doubled, (first, 2, second, 2, 2 * third))
    return doubled.reshape(2 * first, 2 * second, 2 * third)


def smooth(residual, coefficient, level, padder):
    inverse = relax_weight / (6.0 * 0.25 ** level + coefficient)
    guess = inverse * residual
    return guess + inverse * (residual - level_operator(guess, padder(guess), coefficient, level))


def coarse_solve(residual, coefficient):
    inverse = relax_weight / (6.0 * 0.25 ** 3 + coefficient)
    guess = jnp.zeros_like(residual)
    for sweep_index in range(coarse_sweeps):
        guess = guess + inverse * (residual - level_operator(guess, zero_pad(guess), coefficient, 3))
    leftover = residual - level_operator(guess, zero_pad(guess), coefficient, 3)
    ones_field = jnp.ones_like(residual)
    ones_image = level_operator(ones_field, zero_pad(ones_field), coefficient, 3)
    shift = jnp.sum(leftover) / jnp.sum(ones_image)
    return guess + shift


def reference(right_side, diagonal):
    mid_res = restrict(right_side)
    mid_coef = restrict(diagonal)
    low_res = restrict(mid_res)
    low_coef = restrict(mid_coef)
    base_res = restrict(low_res)
    base_coef = restrict(low_coef)
    base_sol = coarse_solve(base_res, base_coef)
    low_sol = smooth(low_res, low_coef, 2, zero_pad) + prolong(base_sol)
    mid_sol = smooth(mid_res, mid_coef, 1, zero_pad) + prolong(low_sol)
    precond = smooth(right_side, diagonal, 0, zero_pad) + prolong(mid_sol)
    image = level_operator(precond, zero_pad(precond), diagonal, 0)
    alpha = jnp.sum(right_side * precond) / jnp.sum(precond * image)
    return alpha * precond, right_side - alpha * image
```

```python
import functools

import jax
import jax.numpy as jnp
from jax import lax
from jax.experimental import pallas as pl
from jax.experimental.pallas import tpu as pltpu
from jax.sharding import PartitionSpec as P

relax_weight = 0.8
coarse_sweeps = 8
MESH = pl.DeviceIdType.MESH
f32 = jnp.float32


def iota(shape, dim):
    return lax.broadcasted_iota(jnp.int32, shape, dim)


def split_dot(value, table):
    high = value.astype(jnp.bfloat16)
    low = (value - high.astype(f32)).astype(jnp.bfloat16)
    return jnp.dot(high, table, preferred_element_type=f32) + jnp.dot(
        low, table, preferred_element_type=f32
    )


def plane_neighbours(plane, below, above):
    rows, lanes = plane.shape
    sub, lane = iota(plane.shape, 0), iota(plane.shape, 1)
    total = jnp.where(sub == 0, below, pltpu.roll(plane, 1, 0))
    total += jnp.where(sub == rows - 1, above, pltpu.roll(plane, rows - 1, 0))
    total += jnp.where(lane == 0, 0.0, pltpu.roll(plane, 1, 1))
    return total + jnp.where(lane == lanes - 1, 0.0, pltpu.roll(plane, lanes - 1, 1))


def kernel(
    n_gx, n_gy, nx, ny, nz,
    rs_hbm, dg_hbm, p_hbm, image_hbm, alpha_ref,
    rs, dg, inv0, g0, q0, p0, im0, ysrc0, ydst0, ysrcq, ydstq,
    pair1, coarse1, inv1, g1, ysrc1, ydst1, dup1,
    pair2, coarse2, inv2, g2, ysrc2, ydst2, dup2,
    pair3, gathered, sol, bands, expanded, sums,
    down0, down1, down_res, down_coef, up0, up1, up3,
    load_sem, store_sem, face_send, face_recv,
    line_send, line_recv, peer_send, peer_recv, twin_send, twin_recv,
    sum_send, sum_recv, sum2_send, sum2_recv,
):
    ax, ay = lax.axis_index("gx"), lax.axis_index("gy")
    chunk = 8
    n_chunks = nx // chunk
    nx1, ny1, nz1 = nx // 2, ny // 2, nz // 2
    nx2, ny2, nz2 = nx // 4, ny // 4, nz // 4
    nx3, ny3, nz3 = nx // 8, ny // 8, nz // 8
    half = n_gx // 2

    def load(part, c):
        source, target = ((rs_hbm, rs), (dg_hbm, dg))[part]
        span = pl.ds(c * chunk, chunk)
        return pltpu.make_async_copy(source.at[span], target.at[span], load_sem.at[part, c])

    for c in range(n_chunks):
        load(0, c).start()
        load(1, c).start()

    barrier = pltpu.get_barrier_semaphore()

    def greet_line(k, carry):
        pl.semaphore_signal(barrier, inc=1, device_id=(ax, lax.rem(ay + k, n_gy)), device_id_type=MESH)
        return carry

    def greet_row(k, carry):
        pl.semaphore_signal(barrier, inc=1, device_id=(lax.rem(ax + k, n_gx), ay), device_id_type=MESH)
        return carry

    lax.fori_loop(1, n_gy, greet_line, 0)
    lax.fori_loop(1, n_gx, greet_row, 0)

    def down_table(ref, offset):
        row, column = iota(ref.shape, 0), iota(ref.shape, 1)
        ref[...] = jnp.where((row >> 1) + offset == column, 0.125, 0.0).astype(jnp.bfloat16)

    def up_table(ref, shift):
        row, column = iota(ref.shape, 0), iota(ref.shape, 1)
        ref[...] = jnp.where(row == (column >> shift), 1.0, 0.0).astype(jnp.bfloat16)

    down_table(down0, 0)
    down_table(down1, 0)
    down_table(down_res, 0)
    down_table(down_coef, nz3)
    up_table(up0, 1)
    up_table(up1, 1)
    up_table(up3, 3)

    sides = (
        (ax > 0, (ax - 1, ay)),
        (ax < n_gx - 1, (ax + 1, ay)),
        (ay > 0, (ax, ay - 1)),
        (ay < n_gy - 1, (ax, ay + 1)),
    )

    def faces(group, field, ysrc, ydst):
        count = ysrc.shape[1]
        pairs = (
            (field.at[1], field.at[count + 1]),
            (field.at[count], field.at[0]),
            (ysrc.at[0], ydst.at[1]),
            (ysrc.at[1], ydst.at[0]),
        )
        copies = []
        for side, (source, target) in enumerate(pairs):
            there, device = sides[side]
            copies.append((there, pltpu.make_async_remote_copy(
                src_ref=source, dst_ref=target,
                send_sem=face_send.at[group, side], recv_sem=face_recv.at[group, side ^ 1],
                device_id=device, device_id_type=MESH,
            )))
        return copies

    def start_faces(copies):
        for there, copy in copies:
            pl.when(there)(copy.start)

    def clear_faces(field, ydst):
        targets = (field.at[0], field.at[field.shape[0] - 1], ydst.at[0], ydst.at[1])
        for (there, _), target in zip(sides, targets):
            @pl.when(jnp.logical_not(there))
            def _():
                target[...] = jnp.zeros(target.shape, f32)

    def wait_faces(group, field, ysrc, ydst):
        count = ysrc.shape[1]
        targets = (field.at[0], field.at[count + 1], ydst.at[0], ydst.at[1])
        for side, target in enumerate(targets):
            there, device = sides[side]
            copy = pltpu.make_async_remote_copy(
                src_ref=target, dst_ref=target,
                send_sem=face_send.at[group, side], recv_sem=face_recv.at[group, side],
                device_id=device, device_id_type=MESH,
            )
            pl.when(there)(copy.wait_recv)

    for field, ydst in ((g0, ydst0), (g1, ydst1), (g2, ydst2), (q0, ydstq)):
        clear_faces(field, ydst)

    def first_chunk(c, carry):
        load(0, c).wait()
        load(1, c).wait()

        def first_pair(k, inner):
            j = c * (chunk // 2) + k
            for i in (2 * j, 2 * j + 1):
                inverse = relax_weight / (6.0 + dg[i])
                guess = inverse * rs[i]
                inv0[i] = inverse
                g0[i + 1] = guess
                ysrc0[0, i] = guess[:1]
                ysrc0[1, i] = guess[ny - 1:]
            both = jnp.concatenate([rs[2 * j] + rs[2 * j + 1], dg[2 * j] + dg[2 * j + 1]], axis=0)
            thin = split_dot(both, down0[...])
            for b in range(nz1 // 128):
                pair1[0, b, j] = thin[:ny, b * 128:(b + 1) * 128]
                pair1[1, b, j] = thin[ny:, b * 128:(b + 1) * 128]
            return inner

        return lax.fori_loop(0, chunk // 2, first_pair, carry)

    lax.fori_loop(0, n_chunks, first_chunk, 0)

    pl.semaphore_wait(barrier, n_gy + n_gx - 2)
    copies0 = faces(0, g0, ysrc0, ydst0)
    start_faces(copies0)

    def mid_pair(j, carry):
        total = []
        for part in range(2):
            total.append(0.0)
            for i in (2 * j, 2 * j + 1):
                coarse1[part, i & 1] = jnp.concatenate([
                    pair1[part, b, i, pl.ds(0, ny1, 2), :] + pair1[part, b, i, pl.ds(1, ny1, 2), :]
                    for b in range(nz1 // 128)
                ], axis=1)
        for i in range(2):
            inverse = relax_weight / (1.5 + coarse1[1, i])
            guess = inverse * coarse1[0, i]
            inv1[2 * j + i] = inverse * 0.25
            g1[2 * j + i + 1] = guess
            ysrc1[0, 2 * j + i] = guess[:1]
            ysrc1[1, 2 * j + i] = guess[ny1 - 1:]
        both = jnp.concatenate(
            [coarse1[0, 0] + coarse1[0, 1], coarse1[1, 0] + coarse1[1, 1]], axis=0)
        thin = split_dot(both, down1[...])
        pair2[0, j] = thin[:ny1]
        pair2[1, j] = thin[ny1:]
        return carry

    lax.fori_loop(0, nx1 // 2, mid_pair, 0)
    copies1 = faces(1, g1, ysrc1, ydst1)
    start_faces(copies1)

    def low_pair(j, carry):
        for part in range(2):
            for i in range(2):
                coarse2[part, 2 * j + i] = (
                    pair2[part, 2 * j + i, pl.ds(0, ny2, 2), :] + pair2[part, 2 * j + i, pl.ds(1, ny2, 2), :])
        for i in range(2):
            inverse = relax_weight / (0.375 + coarse2[1, 2 * j + i])
            guess = inverse * coarse2[0, 2 * j + i]
            inv2[2 * j + i] = inverse * 0.0625
            g2[2 * j + i + 1] = guess
            ysrc2[0, 2 * j + i] = guess[:1]
            ysrc2[1, 2 * j + i] = guess[ny2 - 1:]
        return carry

    lax.fori_loop(0, nx2 // 2, low_pair, 0)
    res_sum = coarse2[0].reshape(nx3, 2, ny2, nz2).sum(axis=1).reshape(nx3 * ny2, nz2)
    coef_sum = coarse2[1].reshape(nx3, 2, ny2, nz2).sum(axis=1).reshape(nx3 * ny2, nz2)
    pair3[...] = split_dot(res_sum, down_res[...]) + split_dot(coef_sum, down_coef[...])
    core, height = ax % 2, ax // 2
    for y in range(ny3):
        gathered[core, height, ay, y] = (
            pair3[pl.ds(2 * y, nx3, ny2), :] + pair3[pl.ds(2 * y + 1, nx3, ny2), :])

    def line_copy(k, slot):
        return pltpu.make_async_remote_copy(
            src_ref=gathered.at[core, height, slot], dst_ref=gathered.at[core, height, slot],
            send_sem=line_send.at[k], recv_sem=line_recv.at[slot],
            device_id=(ax, lax.rem(ay + k, n_gy)), device_id_type=MESH,
        )

    def line_start(k, carry):
        line_copy(k, ay).start()
        return carry

    def line_wait(k, carry):
        line_copy(k, lax.rem(ay + k, n_gy)).wait_recv()
        return carry

    def peer_copy(k, slot):
        return pltpu.make_async_remote_copy(
            src_ref=gathered.at[core, slot], dst_ref=gathered.at[core, slot],
            send_sem=peer_send.at[k], recv_sem=peer_recv.at[slot],
            device_id=(lax.rem(height + k, half) * 2 + core, ay), device_id_type=MESH,
        )

    def twin_copy(slot):
        return pltpu.make_async_remote_copy(
            src_ref=gathered.at[slot], dst_ref=gathered.at[slot],
            send_sem=twin_send.at[0], recv_sem=twin_recv.at[0],
            device_id=(height * 2 + 1 - core, ay), device_id_type=MESH,
        )

    lax.fori_loop(1, n_gy, line_start, 0)
    copies2 = faces(2, g2, ysrc2, ydst2)
    start_faces(copies2)

    wait_faces(2, g2, ysrc2, ydst2)

    def low_smooth(i, carry):
        plane = g2[i + 1]
        total = g2[i] + g2[i + 2] + plane_neighbours(plane, ydst2[0, i], ydst2[1, i])
        smooth = (2.0 - relax_weight) * plane + inv2[i] * total
        dup2[i, pl.ds(0, ny2, 2), :] = smooth
        dup2[i, pl.ds(1, ny2, 2), :] = smooth
        return carry

    lax.fori_loop(0, nx2, low_smooth, 0)
    wait_faces(1, g1, ysrc1, ydst1)

    def mid_smooth(j, carry):
        wide = split_dot(dup2[j], up1[...])
        for i in (2 * j, 2 * j + 1):
            plane = g1[i + 1]
            total = g1[i] + g1[i + 2] + plane_neighbours(plane, ydst1[0, i], ydst1[1, i])
            smooth = (2.0 - relax_weight) * plane + inv1[i] * total + wide
            for b in range(nz1 // 128):
                part = smooth[:, b * 128:(b + 1) * 128]
                dup1[b, i, pl.ds(0, ny1, 2), :] = part
                dup1[b, i, pl.ds(1, ny1, 2), :] = part
        return carry

    lax.fori_loop(0, nx2, mid_smooth, 0)

    lax.fori_loop(1, n_gy, line_wait, 0)
    for k in range(1, half):
        peer_copy(k, height).start()

    wait_faces(0, g0, ysrc0, ydst0)

    def fine_smooth(j, carry):
        source = jnp.concatenate([dup1[b, j] for b in range(nz1 // 128)], axis=1)
        wide = split_dot(source, up0[...])
        for i in (2 * j, 2 * j + 1):
            plane = g0[i + 1]
            total = g0[i] + g0[i + 2] + plane_neighbours(plane, ydst0[0, i], ydst0[1, i])
            smooth = (2.0 - relax_weight) * plane + inv0[i] * total + wide
            q0[i + 1] = smooth
            ysrcq[0, i] = smooth[:1]
            ysrcq[1, i] = smooth[ny - 1:]
        return carry

    lax.fori_loop(0, nx1, fine_smooth, 0)
    copiesq = faces(3, q0, ysrcq, ydstq)
    start_faces(copiesq)

    for k in range(1, half):
        peer_copy(k, lax.rem(height + k, half)).wait_recv()
    twin_copy(core).start()
    twin_copy(1 - core).wait_recv()

    wx3, wy3 = nx3 * n_gx, ny3 * n_gy
    hy3 = wy3 // 2
    lanes = 2 * nz3

    def whole(first):
        return jnp.concatenate([
            gathered[a % 2, a // 2, first:first + n_gy // 2].reshape(hy3, nx3, lanes)
            for a in range(n_gx)
        ], axis=1)

    lower, upper = whole(0), whole(n_gy // 2)
    shape = (hy3, wx3, lanes)
    lane, row, level = iota(shape, 2), iota(shape, 1), iota(shape, 0)
    is_low = lane < nz3
    res3 = jnp.where(is_low, lower, pltpu.roll(upper, nz3, 2))
    coef3 = jnp.where(is_low, pltpu.roll(lower, nz3, 2), upper)
    scale3 = 0.25**3
    inverse3 = relax_weight / (6.0 * scale3 + coef3)
    step3 = inverse3 * scale3
    guess3 = inverse3 * res3
    depth = jnp.where(is_low, lane, lane - nz3)
    no_left, no_right = depth == 0, depth == nz3 - 1
    no_down, no_up = row == 0, row == wx3 - 1
    flat_low = iota((1, wx3, lanes), 2) < nz3

    def coarse_neighbours(field):
        first = jnp.where(flat_low, 0.0, pltpu.roll(field[hy3 - 1:], nz3, 2))
        last = jnp.where(flat_low, pltpu.roll(field[:1], nz3, 2), 0.0)
        total = jnp.concatenate([first, field[:hy3 - 1]], axis=0)
        total += jnp.concatenate([field[1:], last], axis=0)
        total += jnp.where(no_down, 0.0, pltpu.roll(field, 1, 1))
        total += jnp.where(no_up, 0.0, pltpu.roll(field, wx3 - 1, 1))
        total += jnp.where(no_left, 0.0, pltpu.roll(field, 1, 2))
        return total + jnp.where(no_right, 0.0, pltpu.roll(field, lanes - 1, 2))

    jac = guess3
    for _ in range(coarse_sweeps - 1):
        jac = (1.0 - relax_weight) * jac + guess3 + step3 * coarse_neighbours(jac)

    def one(flag):
        return jnp.where(flag, 1.0, 0.0)

    ends = one(no_left) + one(no_right) + one(no_down) + one(no_up)
    ends += one(jnp.logical_and(level == 0, is_low))
    ends += one(jnp.logical_and(level == hy3 - 1, jnp.logical_not(is_low)))
    ones_image = scale3 * ends + coef3
    shift = jnp.sum(res3 - ones_image * jac) / jnp.sum(ones_image)
    jac = jac + shift

    sol[...] = jnp.zeros(sol.shape, f32)
    sol[1:hy3 + 1, nx3:nx3 + wx3, :] = jnp.where(is_low, jac, 0.0)
    sol[hy3 + 1:wy3 + 1, nx3:nx3 + wx3, :] = jnp.where(is_low, pltpu.roll(jac, nz3, 2), 0.0)

    near = sol[pl.ds(ay * ny3, ny3 + 2), pl.ds(pl.multiple_of(ax * nx3, nx3), 3 * nx3), :]
    wide = split_dot(near.reshape((ny3 + 2) * 3 * nx3, lanes), up3[...])
    expanded[...] = wide.reshape(ny3 + 2, 3 * nx3, nz)
    for y in range(ny3):
        around = expanded[y + 1]
        own = around[nx3:2 * nx3]
        column = iota(own.shape, 1)
        bands[0, y] = own
        bands[1, y] = (
            2.0 * own
            - jnp.where(column == 0, 0.0, pltpu.roll(own, 1, 1))
            - jnp.where(column == nz - 1, 0.0, pltpu.roll(own, nz - 1, 1)))
        bands[2, y] = own - expanded[y, nx3:2 * nx3]
        bands[3, y] = own - expanded[y + 2, nx3:2 * nx3]
        bands[4, y] = own - pltpu.roll(around, 1, 0)[nx3:2 * nx3]
        bands[5, y] = own - pltpu.roll(around, 3 * nx3 - 1, 0)[nx3:2 * nx3]

    wait_faces(3, q0, ysrcq, ydstq)

    def store(part, c):
        source, target = ((p0, p_hbm), (im0, image_hbm))[part]
        span = pl.ds(c * chunk, chunk)
        return pltpu.make_async_copy(source.at[span], target.at[span], store_sem.at[part, c])

    fold = ny // ny3

    def fold_plane(value):
        total = value.reshape(ny // 8, 8, nz).sum(axis=0)
        return sum(total[:, b * 128:(b + 1) * 128] for b in range(nz // 128))

    def last_chunk(c, carry):
        def rows(kind):
            return [
                jnp.broadcast_to(bands[kind, y, pl.ds(c, 1), :], (fold, nz)) for y in range(ny3)]

        def laid(parts):
            return jnp.concatenate(parts, axis=0)

        sub = iota((fold, nz), 0)
        own = laid(rows(0))
        edge = laid([
            flat + jnp.where(sub == 0, down, 0.0) + jnp.where(sub == fold - 1, up, 0.0)
            for flat, down, up in zip(rows(1), rows(2), rows(3))])
        rz, zq = carry
        for k in range(chunk):
            i = c * chunk + k
            plane = q0[i + 1]
            near_sum = q0[i] + q0[i + 2] + plane_neighbours(plane, ydstq[0, i], ydstq[1, i])
            precond = plane + own
            image = 6.0 * plane - near_sum + dg[i] * precond + edge
            if k == 0:
                image += laid(rows(4))
            if k == chunk - 1:
                image += laid(rows(5))
            p0[i] = precond
            im0[i] = image
            rz += fold_plane(rs[i] * precond)
            zq += fold_plane(precond * image)
        store(0, c).start()
        store(1, c).start()
        return rz, zq

    zero = jnp.zeros((8, 128), f32)
    rz, zq = lax.fori_loop(0, n_chunks, last_chunk, (zero, zero))

    def sum_copy(k, slot):
        return pltpu.make_async_remote_copy(
            src_ref=sums.at[slot], dst_ref=sums.at[slot],
            send_sem=sum_send.at[k], recv_sem=sum_recv.at[slot],
            device_id=(ax, lax.rem(ay + k, n_gy)), device_id_type=MESH,
        )

    def sum2_copy(k, slot):
        return pltpu.make_async_remote_copy(
            src_ref=sums.at[n_gy + slot], dst_ref=sums.at[n_gy + slot],
            send_sem=sum2_send.at[k], recv_sem=sum2_recv.at[slot],
            device_id=(lax.rem(ax + k, n_gx), ay), device_id_type=MESH,
        )

    sums[ay] = jnp.concatenate(
        [rz.sum(axis=0, keepdims=True), zq.sum(axis=0, keepdims=True)], axis=0)
    for k in range(1, n_gy):
        sum_copy(k, ay).start()
    for k in range(1, n_gy):
        sum_copy(k, lax.rem(ay + k, n_gy)).wait_recv()
    sums[n_gy + ax] = sum(sums[k] for k in range(n_gy))
    for k in range(1, n_gx):
        sum2_copy(k, ax).start()
    for k in range(1, n_gx):
        sum2_copy(k, lax.rem(ax + k, n_gx)).wait_recv()
    total = sum(sums[n_gy + k] for k in range(n_gx))
    both = jnp.sum(total, axis=1, keepdims=True)
    alpha_ref[...] = jnp.broadcast_to(both[:1] / both[1:], alpha_ref.shape)

    def store_wait(c, carry):
        store(0, c).wait()
        store(1, c).wait()
        return carry

    lax.fori_loop(0, n_chunks, store_wait, 0)
    for copies in (copies0, copies1, copies2, copiesq):
        for there, copy in copies:
            pl.when(there)(copy.wait_send)

    def line_sent(k, carry):
        line_copy(k, ay).wait_send()
        return carry

    lax.fori_loop(1, n_gy, line_sent, 0)
    for k in range(1, half):
        peer_copy(k, height).wait_send()
    twin_copy(core).wait_send()
    for k in range(1, n_gy):
        sum_copy(k, ay).wait_send()
    for k in range(1, n_gx):
        sum2_copy(k, ax).wait_send()


def body(right_side, diagonal):
    n_gx, n_gy = lax.axis_size("gx"), lax.axis_size("gy")
    nx, ny, nz = right_side.shape
    V = lambda *shape: pltpu.VMEM(shape, f32)
    B = lambda *shape: pltpu.VMEM(shape, jnp.bfloat16)
    D = lambda *shape: pltpu.SemaphoreType.DMA(shape)
    nx1, ny1, nz1 = nx // 2, ny // 2, nz // 2
    nx2, ny2, nz2 = nx // 4, ny // 4, nz // 4
    nx3, ny3, nz3 = nx // 8, ny // 8, nz // 8
    block = V(nx, ny, nz)
    scratch = [
        block, block, block, V(nx + 2, ny, nz), V(nx + 2, ny, nz), block, block,
        V(2, nx, 1, nz), V(2, nx, 1, nz), V(2, nx, 1, nz), V(2, nx, 1, nz),
        V(2, nz1 // 128, nx1, ny, 128), V(2, 2, ny1, nz1), V(nx1, ny1, nz1), V(nx1 + 2, ny1, nz1),
        V(2, nx1, 1, nz1), V(2, nx1, 1, nz1), V(nz1 // 128, nx1, ny, 128),
        V(2, nx2, ny1, nz2), V(2, nx2, ny2, nz2), V(nx2, ny2, nz2), V(nx2 + 2, ny2, nz2),
        V(2, nx2, 1, nz2), V(2, nx2, 1, nz2), V(nx2, ny1, nz2),
        V(nx3 * ny2, 2 * nz3), V(2, n_gx // 2, n_gy, ny3, nx3, 2 * nz3),
        V(ny3 * n_gy + 2, nx3 * (n_gx + 2), 2 * nz3), V(6, ny3, nx3, nz), V(ny3 + 2, 3 * nx3, nz),
        V(n_gx + n_gy, 2, 128),
        B(nz, nz1), B(nz1, nz2), B(nz2, 2 * nz3), B(nz2, 2 * nz3),
        B(nz1, nz), B(nz2, nz1), B(2 * nz3, nz),
        D(2, nx // 8), D(2, nx // 8), D(4, 4), D(4, 4),
        D(n_gy), D(n_gy), D(n_gx), D(n_gx), D(1), D(1),
        D(n_gy), D(n_gy), D(n_gx), D(n_gx),
    ]
    whole = jax.ShapeDtypeStruct(right_side.shape, f32)
    precond, image, alpha = pl.pallas_call(
        functools.partial(kernel, n_gx, n_gy, nx, ny, nz),
        out_shape=(whole, whole, jax.ShapeDtypeStruct((8, 128), f32)),
        in_specs=[pl.BlockSpec(memory_space=pl.ANY)] * 2,
        out_specs=(
            pl.BlockSpec(memory_space=pl.ANY), pl.BlockSpec(memory_space=pl.ANY),
            pl.BlockSpec(memory_space=pltpu.VMEM)),
        scratch_shapes=scratch,
        compiler_params=pltpu.CompilerParams(
            collective_id=0, has_side_effects=True, vmem_limit_bytes=48 * 1024 * 1024),
        name="cycle",
    )(right_side, diagonal)
    alpha = alpha[0, 0]
    return alpha * precond, right_side - alpha * image


def solution(mesh):
    placed = (P("gx", "gy", None), P("gx", "gy", None))
    return jax.shard_map(
        body,
        mesh=mesh,
        in_specs=placed,
        out_specs=(P("gx", "gy", None), P("gx", "gy", None)),
        check_vma=False,
    )
```

```python
import functools

import jax
import jax.numpy as jnp
from jax import lax
from jax.experimental import pallas as pl
from jax.experimental.pallas import tpu as pltpu
from jax.sharding import PartitionSpec as P

relax_weight = 0.8
coarse_sweeps = 8
MESH = pl.DeviceIdType.MESH
f32 = jnp.float32


def iota(shape, dim):
    return lax.broadcasted_iota(jnp.int32, shape, dim)


def inverse_of(value):
    guess = pl.reciprocal(value, approx=True)
    return guess * (2.0 * relax_weight - relax_weight * value * guess)


def split_dot(value, table):
    rows = value.shape[0]
    high = value.astype(jnp.bfloat16)
    low = (value - high.astype(f32)).astype(jnp.bfloat16)
    both = jnp.dot(jnp.concatenate([high, low], axis=0), table, preferred_element_type=f32)
    return both[:rows] + both[rows:]


def plane_neighbours(plane, below, above):
    rows, lanes = plane.shape
    sub, lane = iota((8, 128), 0), iota((8, 128), 1)
    n_rows, n_lanes = rows // 8, lanes // 128
    tiles = [
        [plane[r * 8:r * 8 + 8, b * 128:b * 128 + 128] for b in range(n_lanes)]
        for r in range(n_rows)]
    lower = [[pltpu.roll(tile, 1, 0) for tile in line] for line in tiles]
    upper = [[pltpu.roll(tile, 7, 0) for tile in line] for line in tiles]
    total = []
    for r in range(n_rows):
        left = [pltpu.roll(tile, 1, 1) for tile in tiles[r]]
        right = [pltpu.roll(tile, 127, 1) for tile in tiles[r]]
        line = []
        for b in range(n_lanes):
            edge = slice(b * 128, b * 128 + 128)
            low = lower[r - 1][b] if r else below[:, edge]
            high = upper[r + 1][b] if r < n_rows - 1 else above[:, edge]
            far_left = left[b - 1] if b else 0.0
            far_right = right[b + 1] if b < n_lanes - 1 else 0.0
            line.append(
                (jnp.where(sub == 0, low, lower[r][b]) + jnp.where(sub == 7, high, upper[r][b]))
                + (jnp.where(lane == 0, far_left, left[b])
                   + jnp.where(lane == 127, far_right, right[b])))
        total.append(jnp.concatenate(line, axis=1) if n_lanes > 1 else line[0])
    return jnp.concatenate(total, axis=0) if n_rows > 1 else total[0]


def kernel(
    n_gx, n_gy, nx, ny, nz,
    rs_hbm, dg_hbm, p_hbm, image_hbm, alpha_ref,
    rs, dg, inv0, g0, q0, p0, im0, ysrc0, ydst0, ysrcq, ydstq,
    pair1, inv1, g1, ysrc1, ydst1, dup1,
    pair2, inv2, g2, ysrc2, ydst2, dup2,
    pair3, gathered, sol, bands, expanded, sums,
    down0, down1, up0, up1, up3,
    load_sem, store_sem, face_send, face_recv,
    line_send, line_recv, peer_send, peer_recv, twin_send, twin_recv,
    sum_send, sum_recv, sum2_send, sum2_recv,
):
    ax, ay = lax.axis_index("gx"), lax.axis_index("gy")
    chunk = 8
    n_chunks = nx // chunk
    nx1, ny1, nz1 = nx // 2, ny // 2, nz // 2
    nx2, ny2, nz2 = nx // 4, ny // 4, nz // 4
    nx3, ny3, nz3 = nx // 8, ny // 8, nz // 8
    half = n_gx // 2

    def load(part, c):
        source, target = ((rs_hbm, rs), (dg_hbm, dg))[part]
        span = pl.ds(c * chunk, chunk)
        return pltpu.make_async_copy(source.at[span], target.at[span], load_sem.at[part, c])

    for c in range(n_chunks):
        load(0, c).start()
        load(1, c).start()

    barrier = pltpu.get_barrier_semaphore()

    def greet_line(k, carry):
        pl.semaphore_signal(barrier, inc=1, device_id=(ax, lax.rem(ay + k, n_gy)), device_id_type=MESH)
        return carry

    def greet_row(k, carry):
        pl.semaphore_signal(barrier, inc=1, device_id=(lax.rem(ax + k, n_gx), ay), device_id_type=MESH)
        return carry

    lax.fori_loop(1, n_gy, greet_line, 0)
    lax.fori_loop(1, n_gx, greet_row, 0)

    def down_table(ref):
        row, column = iota(ref.shape, 0), iota(ref.shape, 1)
        ref[...] = jnp.where((row >> 1) == column, 0.125, 0.0).astype(jnp.bfloat16)

    def up_table(ref, shift):
        row, column = iota(ref.shape, 0), iota(ref.shape, 1)
        ref[...] = jnp.where(row == (column >> shift), 1.0, 0.0).astype(jnp.bfloat16)

    down_table(down0)
    down_table(down1)
    up_table(up0, 1)
    up_table(up1, 1)
    up_table(up3, 3)
    sol[...] = jnp.zeros(sol.shape, f32)

    sides = (
        (ax > 0, (ax - 1, ay)),
        (ax < n_gx - 1, (ax + 1, ay)),
        (ay > 0, (ax, ay - 1)),
        (ay < n_gy - 1, (ax, ay + 1)),
    )

    def faces(group, field, ysrc, ydst):
        count = ysrc.shape[1]
        pairs = (
            (field.at[1], field.at[count + 1]),
            (field.at[count], field.at[0]),
            (ysrc.at[0], ydst.at[1]),
            (ysrc.at[1], ydst.at[0]),
        )
        copies = []
        for side, (source, target) in enumerate(pairs):
            there, device = sides[side]
            copies.append((there, pltpu.make_async_remote_copy(
                src_ref=source, dst_ref=target,
                send_sem=face_send.at[group, side], recv_sem=face_recv.at[group, side ^ 1],
                device_id=device, device_id_type=MESH,
            )))
        return copies

    def start_faces(copies):
        for there, copy in copies:
            pl.when(there)(copy.start)

    def clear_faces(field, ydst):
        targets = (field.at[0], field.at[field.shape[0] - 1], ydst.at[0], ydst.at[1])
        for (there, _), target in zip(sides, targets):
            @pl.when(jnp.logical_not(there))
            def _():
                target[...] = jnp.zeros(target.shape, f32)

    def wait_faces(group, field, ysrc, ydst):
        count = ysrc.shape[1]
        targets = (field.at[0], field.at[count + 1], ydst.at[0], ydst.at[1])
        for side, target in enumerate(targets):
            there, device = sides[side]
            copy = pltpu.make_async_remote_copy(
                src_ref=target, dst_ref=target,
                send_sem=face_send.at[group, side], recv_sem=face_recv.at[group, side],
                device_id=device, device_id_type=MESH,
            )
            pl.when(there)(copy.wait_recv)

    for field, ydst in ((g0, ydst0), (g1, ydst1), (g2, ydst2), (q0, ydstq)):
        clear_faces(field, ydst)

    def first_chunk(c, carry):
        load(0, c).wait()
        load(1, c).wait()

        stacked = []
        for k in range(chunk // 2):
            j = c * (chunk // 2) + k
            for i in (2 * j, 2 * j + 1):
                inverse = inverse_of(6.0 + dg[i])
                guess = inverse * rs[i]
                inv0[i] = inverse
                g0[i + 1] = guess
                ysrc0[0, i] = guess[:1]
                ysrc0[1, i] = guess[ny - 1:]
            stacked += [rs[2 * j] + rs[2 * j + 1], dg[2 * j] + dg[2 * j + 1]]
        thin = split_dot(jnp.concatenate(stacked, axis=0), down0[...])
        for k in range(chunk // 2):
            for part in range(2):
                first = (2 * k + part) * ny
                for b in range(nz1 // 128):
                    pair1[part, b, c * (chunk // 2) + k] = thin[first:first + ny, b * 128:(b + 1) * 128]
        return carry

    lax.fori_loop(0, n_chunks, first_chunk, 0)

    pl.semaphore_wait(barrier, n_gy + n_gx - 2)
    copies0 = faces(0, g0, ysrc0, ydst0)
    start_faces(copies0)

    group = min(16, nx1)

    def mid_group(h, carry):
        def halved(part, i):
            return jnp.concatenate([
                pair1[part, b, i, pl.ds(0, ny1, 2), :] + pair1[part, b, i, pl.ds(1, ny1, 2), :]
                for b in range(nz1 // 128)
            ], axis=1)

        stacked = []
        for k in range(group // 2):
            planes = []
            for i in (h * group + 2 * k, h * group + 2 * k + 1):
                res, coef = halved(0, i), halved(1, i)
                inverse = inverse_of(1.5 + coef)
                guess = inverse * res
                inv1[i] = inverse * 0.25
                g1[i + 1] = guess
                ysrc1[0, i] = guess[:1]
                ysrc1[1, i] = guess[ny1 - 1:]
                planes.append((res, coef))
            stacked += [planes[0][0] + planes[1][0], planes[0][1] + planes[1][1]]
        thin = split_dot(jnp.concatenate(stacked, axis=0), down1[...])
        for k in range(group // 2):
            for part in range(2):
                first = (2 * k + part) * ny1
                pair2[part, h * (group // 2) + k] = thin[first:first + ny1]
        return carry

    lax.fori_loop(0, nx1 // group, mid_group, 0)
    copies1 = faces(1, g1, ysrc1, ydst1)
    start_faces(copies1)

    low = []
    for i in range(nx2):
        res, coef = (
            pair2[part, i, pl.ds(0, ny2, 2), :] + pair2[part, i, pl.ds(1, ny2, 2), :]
            for part in range(2))
        inverse = inverse_of(0.375 + coef)
        guess = inverse * res
        inv2[i] = inverse * 0.0625
        g2[i + 1] = guess
        ysrc2[0, i] = guess[:1]
        ysrc2[1, i] = guess[ny2 - 1:]
        low.append((res, coef))
    stacked = [
        jnp.concatenate([low[2 * k][part] + low[2 * k + 1][part] for part in range(2)], axis=1)
        for k in range(nx3)]
    pair3[...] = split_dot(jnp.concatenate(stacked, axis=0), down1[...])
    core, height = ax % 2, ax // 2
    for y in range(ny3):
        gathered[core, height, ay, y] = (
            pair3[pl.ds(2 * y, nx3, ny2), :] + pair3[pl.ds(2 * y + 1, nx3, ny2), :])

    def line_copy(k, slot):
        return pltpu.make_async_remote_copy(
            src_ref=gathered.at[core, height, slot], dst_ref=gathered.at[core, height, slot],
            send_sem=line_send.at[k], recv_sem=line_recv.at[slot],
            device_id=(ax, lax.rem(ay + k, n_gy)), device_id_type=MESH,
        )

    def line_start(k, carry):
        line_copy(k, ay).start()
        return carry

    def line_wait(k, carry):
        line_copy(k, lax.rem(ay + k, n_gy)).wait_recv()
        return carry

    def peer_copy(k, slot):
        return pltpu.make_async_remote_copy(
            src_ref=gathered.at[core, slot], dst_ref=gathered.at[core, slot],
            send_sem=peer_send.at[k], recv_sem=peer_recv.at[slot],
            device_id=(lax.rem(height + k, half) * 2 + core, ay), device_id_type=MESH,
        )

    def twin_copy(slot):
        return pltpu.make_async_remote_copy(
            src_ref=gathered.at[slot], dst_ref=gathered.at[slot],
            send_sem=twin_send.at[0], recv_sem=twin_recv.at[0],
            device_id=(height * 2 + 1 - core, ay), device_id_type=MESH,
        )

    lax.fori_loop(1, n_gy, line_start, 0)
    copies2 = faces(2, g2, ysrc2, ydst2)
    start_faces(copies2)

    wait_faces(0, g0, ysrc0, ydst0)

    def fine_smooth(c, carry):
        for k in range(chunk):
            i = c * chunk + k
            plane = g0[i + 1]
            total = g0[i] + g0[i + 2] + plane_neighbours(plane, ydst0[0, i], ydst0[1, i])
            q0[i + 1] = (2.0 - relax_weight) * plane + inv0[i] * total
        return carry

    lax.fori_loop(0, n_chunks, fine_smooth, 0)

    lax.fori_loop(1, n_gy, line_wait, 0)
    for k in range(1, half):
        peer_copy(k, height).start()

    wait_faces(2, g2, ysrc2, ydst2)
    for i in range(nx2):
        plane = g2[i + 1]
        total = g2[i] + g2[i + 2] + plane_neighbours(plane, ydst2[0, i], ydst2[1, i])
        smooth = (2.0 - relax_weight) * plane + inv2[i] * total
        dup2[i, pl.ds(0, ny2, 2), :] = smooth
        dup2[i, pl.ds(1, ny2, 2), :] = smooth

    wait_faces(1, g1, ysrc1, ydst1)

    def mid_smooth(h, carry):
        source = dup2[pl.ds(h * (group // 2), group // 2)]
        wide = split_dot(source.reshape(group // 2 * ny1, nz2), up1[...])
        for k in range(group):
            i = h * group + k
            plane = g1[i + 1]
            total = g1[i] + g1[i + 2] + plane_neighbours(plane, ydst1[0, i], ydst1[1, i])
            smooth = (2.0 - relax_weight) * plane + inv1[i] * total
            smooth += wide[k // 2 * ny1:(k // 2 + 1) * ny1]
            for b in range(nz1 // 128):
                part = smooth[:, b * 128:(b + 1) * 128]
                dup1[b, i, pl.ds(0, ny1, 2), :] = part
                dup1[b, i, pl.ds(1, ny1, 2), :] = part
        return carry

    lax.fori_loop(0, nx1 // group, mid_smooth, 0)

    for k in range(1, half):
        peer_copy(k, lax.rem(height + k, half)).wait_recv()
    twin_copy(core).start()

    def carry_up(c, carry):
        span = pl.ds(c * (chunk // 2), chunk // 2)
        source = jnp.concatenate(
            [dup1[b, span].reshape(chunk // 2 * ny, 128) for b in range(nz1 // 128)], axis=1)
        wide = split_dot(source, up0[...])
        for k in range(chunk):
            i = c * chunk + k
            smooth = q0[i + 1] + wide[k // 2 * ny:(k // 2 + 1) * ny]
            q0[i + 1] = smooth
            ysrcq[0, i] = smooth[:1]
            ysrcq[1, i] = smooth[ny - 1:]
        return carry

    lax.fori_loop(0, n_chunks, carry_up, 0)
    copiesq = faces(3, q0, ysrcq, ydstq)
    start_faces(copiesq)

    twin_copy(1 - core).wait_recv()

    wx3, wy3 = nx3 * n_gx, ny3 * n_gy
    hy3 = wy3 // 2
    lanes = 2 * nz3

    def whole(first):
        return jnp.concatenate([
            gathered[a % 2, a // 2, first:first + n_gy // 2].reshape(hy3, nx3, lanes)
            for a in range(n_gx)
        ], axis=1)

    lower, upper = whole(0), whole(n_gy // 2)
    shape = (hy3, wx3, lanes)
    lane, row, level = iota(shape, 2), iota(shape, 1), iota(shape, 0)
    is_low = lane < nz3
    res3 = jnp.where(is_low, lower, pltpu.roll(upper, nz3, 2))
    coef3 = jnp.where(is_low, pltpu.roll(lower, nz3, 2), upper)
    scale3 = 0.25**3
    inverse3 = relax_weight / (6.0 * scale3 + coef3)
    step3 = inverse3 * scale3
    guess3 = inverse3 * res3
    depth = jnp.where(is_low, lane, lane - nz3)
    no_left, no_right = depth == 0, depth == nz3 - 1
    no_down, no_up = row == 0, row == wx3 - 1
    flat_low = iota((1, wx3, lanes), 2) < nz3

    def coarse_neighbours(field):
        first = jnp.where(flat_low, 0.0, pltpu.roll(field[hy3 - 1:], nz3, 2))
        last = jnp.where(flat_low, pltpu.roll(field[:1], nz3, 2), 0.0)
        total = jnp.concatenate([first, field[:hy3 - 1]], axis=0)
        total += jnp.concatenate([field[1:], last], axis=0)
        total += jnp.where(no_down, 0.0, pltpu.roll(field, 1, 1))
        total += jnp.where(no_up, 0.0, pltpu.roll(field, wx3 - 1, 1))
        total += jnp.where(no_left, 0.0, pltpu.roll(field, 1, 2))
        return total + jnp.where(no_right, 0.0, pltpu.roll(field, lanes - 1, 2))

    jac = guess3
    for _ in range(coarse_sweeps - 1):
        jac = (1.0 - relax_weight) * jac + guess3 + step3 * coarse_neighbours(jac)

    def one(flag):
        return jnp.where(flag, 1.0, 0.0)

    ends = one(no_left) + one(no_right) + one(no_down) + one(no_up)
    ends += one(jnp.logical_and(level == 0, is_low))
    ends += one(jnp.logical_and(level == hy3 - 1, jnp.logical_not(is_low)))
    ones_image = scale3 * ends + coef3
    shift = jnp.sum(res3 - ones_image * jac) / jnp.sum(ones_image)
    jac = jac + shift

    sol[1:hy3 + 1, nx3:nx3 + wx3, :] = jnp.where(is_low, jac, 0.0)
    sol[hy3 + 1:wy3 + 1, nx3:nx3 + wx3, :] = jnp.where(is_low, pltpu.roll(jac, nz3, 2), 0.0)

    near = sol[pl.ds(ay * ny3, ny3 + 2), pl.ds(pl.multiple_of(ax * nx3, nx3), 3 * nx3), :]
    wide = split_dot(near.reshape((ny3 + 2) * 3 * nx3, lanes), up3[...])
    expanded[...] = wide.reshape(ny3 + 2, 3 * nx3, nz)
    for y in range(ny3):
        around = expanded[y + 1]
        own = around[nx3:2 * nx3]
        column = iota(own.shape, 1)
        bands[0, y] = own
        bands[1, y] = (
            2.0 * own
            - jnp.where(column == 0, 0.0, pltpu.roll(own, 1, 1))
            - jnp.where(column == nz - 1, 0.0, pltpu.roll(own, nz - 1, 1)))
        bands[2, y] = own - expanded[y, nx3:2 * nx3]
        bands[3, y] = own - expanded[y + 2, nx3:2 * nx3]
        bands[4, y] = own - pltpu.roll(around, 1, 0)[nx3:2 * nx3]
        bands[5, y] = own - pltpu.roll(around, 3 * nx3 - 1, 0)[nx3:2 * nx3]

    wait_faces(3, q0, ysrcq, ydstq)

    def store(part, c):
        source, target = ((p0, p_hbm), (im0, image_hbm))[part]
        span = pl.ds(c * chunk, chunk)
        return pltpu.make_async_copy(source.at[span], target.at[span], store_sem.at[part, c])

    fold = ny // ny3

    def fold_plane(value):
        total = value.reshape(ny // 8, 8, nz).sum(axis=0)
        return sum(total[:, b * 128:(b + 1) * 128] for b in range(nz // 128))

    def last_chunk(c, carry):
        def rows(kind):
            return [
                jnp.broadcast_to(bands[kind, y, pl.ds(c, 1), :], (fold, nz)) for y in range(ny3)]

        def laid(parts):
            return jnp.concatenate(parts, axis=0)

        sub = iota((fold, nz), 0)
        own = laid(rows(0))
        edge = laid([
            flat + jnp.where(sub == 0, down, 0.0) + jnp.where(sub == fold - 1, up, 0.0)
            for flat, down, up in zip(rows(1), rows(2), rows(3))])
        rz, zq = carry
        for k in range(chunk):
            i = c * chunk + k
            plane = q0[i + 1]
            near_sum = q0[i] + q0[i + 2] + plane_neighbours(plane, ydstq[0, i], ydstq[1, i])
            precond = plane + own
            image = 6.0 * plane - near_sum + dg[i] * precond + edge
            if k == 0:
                image += laid(rows(4))
            if k == chunk - 1:
                image += laid(rows(5))
            p0[i] = precond
            im0[i] = image
            rz += fold_plane(rs[i] * precond)
            zq += fold_plane(precond * image)
        store(0, c).start()
        store(1, c).start()
        return rz, zq

    zero = jnp.zeros((8, 128), f32)
    rz, zq = lax.fori_loop(0, n_chunks, last_chunk, (zero, zero))

    def sum_copy(k, slot):
        return pltpu.make_async_remote_copy(
            src_ref=sums.at[slot], dst_ref=sums.at[slot],
            send_sem=sum_send.at[k], recv_sem=sum_recv.at[slot],
            device_id=(ax, lax.rem(ay + k, n_gy)), device_id_type=MESH,
        )

    def sum2_copy(k, slot):
        return pltpu.make_async_remote_copy(
            src_ref=sums.at[n_gy + slot], dst_ref=sums.at[n_gy + slot],
            send_sem=sum2_send.at[k], recv_sem=sum2_recv.at[slot],
            device_id=(lax.rem(ax + k, n_gx), ay), device_id_type=MESH,
        )

    sums[ay] = jnp.concatenate(
        [rz.sum(axis=0, keepdims=True), zq.sum(axis=0, keepdims=True)], axis=0)
    for k in range(1, n_gy):
        sum_copy(k, ay).start()
    for k in range(1, n_gy):
        sum_copy(k, lax.rem(ay + k, n_gy)).wait_recv()
    sums[n_gy + ax] = sum(sums[k] for k in range(n_gy))
    for k in range(1, n_gx):
        sum2_copy(k, ax).start()
    for k in range(1, n_gx):
        sum2_copy(k, lax.rem(ax + k, n_gx)).wait_recv()
    total = sum(sums[n_gy + k] for k in range(n_gx))
    both = jnp.sum(total, axis=1, keepdims=True)
    alpha_ref[...] = jnp.broadcast_to(both[:1] / both[1:], alpha_ref.shape)

    def store_wait(c, carry):
        store(0, c).wait()
        store(1, c).wait()
        return carry

    lax.fori_loop(0, n_chunks, store_wait, 0)
    for copies in (copies0, copies1, copies2, copiesq):
        for there, copy in copies:
            pl.when(there)(copy.wait_send)

    def line_sent(k, carry):
        line_copy(k, ay).wait_send()
        return carry

    lax.fori_loop(1, n_gy, line_sent, 0)
    for k in range(1, half):
        peer_copy(k, height).wait_send()
    twin_copy(core).wait_send()
    for k in range(1, n_gy):
        sum_copy(k, ay).wait_send()
    for k in range(1, n_gx):
        sum2_copy(k, ax).wait_send()


def body(right_side, diagonal):
    n_gx, n_gy = lax.axis_size("gx"), lax.axis_size("gy")
    nx, ny, nz = right_side.shape
    V = lambda *shape: pltpu.VMEM(shape, f32)
    B = lambda *shape: pltpu.VMEM(shape, jnp.bfloat16)
    D = lambda *shape: pltpu.SemaphoreType.DMA(shape)
    nx1, ny1, nz1 = nx // 2, ny // 2, nz // 2
    nx2, ny2, nz2 = nx // 4, ny // 4, nz // 4
    nx3, ny3, nz3 = nx // 8, ny // 8, nz // 8
    block = V(nx, ny, nz)
    scratch = [
        block, block, block, V(nx + 2, ny, nz), V(nx + 2, ny, nz), block, block,
        V(2, nx, 1, nz), V(2, nx, 1, nz), V(2, nx, 1, nz), V(2, nx, 1, nz),
        V(2, nz1 // 128, nx1, ny, 128), V(nx1, ny1, nz1), V(nx1 + 2, ny1, nz1),
        V(2, nx1, 1, nz1), V(2, nx1, 1, nz1), V(nz1 // 128, nx1, ny, 128),
        V(2, nx2, ny1, nz2), V(nx2, ny2, nz2), V(nx2 + 2, ny2, nz2),
        V(2, nx2, 1, nz2), V(2, nx2, 1, nz2), V(nx2, ny1, nz2),
        V(nx3 * ny2, 2 * nz3), V(2, n_gx // 2, n_gy, ny3, nx3, 2 * nz3),
        V(ny3 * n_gy + 2, nx3 * (n_gx + 2), 2 * nz3), V(6, ny3, nx3, nz), V(ny3 + 2, 3 * nx3, nz),
        V(n_gx + n_gy, 2, 128),
        B(nz, nz1), B(nz1, nz2),
        B(nz1, nz), B(nz2, nz1), B(2 * nz3, nz),
        D(2, nx // 8), D(2, nx // 8), D(4, 4), D(4, 4),
        D(n_gy), D(n_gy), D(n_gx), D(n_gx), D(1), D(1),
        D(n_gy), D(n_gy), D(n_gx), D(n_gx),
    ]
    whole = jax.ShapeDtypeStruct(right_side.shape, f32)
    precond, image, alpha = pl.pallas_call(
        functools.partial(kernel, n_gx, n_gy, nx, ny, nz),
        out_shape=(whole, whole, jax.ShapeDtypeStruct((8, 128), f32)),
        in_specs=[pl.BlockSpec(memory_space=pl.ANY)] * 2,
        out_specs=(
            pl.BlockSpec(memory_space=pl.ANY), pl.BlockSpec(memory_space=pl.ANY),
            pl.BlockSpec(memory_space=pltpu.VMEM)),
        scratch_shapes=scratch,
        compiler_params=pltpu.CompilerParams(
            collective_id=0, has_side_effects=True, vmem_limit_bytes=48 * 1024 * 1024),
        name="cycle",
    )(right_side, diagonal)
    alpha = alpha[0, 0]
    return alpha * precond, right_side - alpha * image


def solution(mesh):
    placed = (P("gx", "gy", None), P("gx", "gy", None))
    return jax.shard_map(
        body,
        mesh=mesh,
        in_specs=placed,
        out_specs=(P("gx", "gy", None), P("gx", "gy", None)),
        check_vma=False,
    )
```

```python
import functools

import jax
import jax.numpy as jnp
from jax import lax
from jax.experimental import pallas as pl
from jax.experimental.pallas import tpu as pltpu
from jax.sharding import PartitionSpec as P

relax_weight = 0.8
coarse_sweeps = 8
MESH = pl.DeviceIdType.MESH
f32 = jnp.float32


def iota(shape, dim):
    return lax.broadcasted_iota(jnp.int32, shape, dim)


def inverse_of(value):
    guess = pl.reciprocal(value, approx=True)
    return guess * (2.0 * relax_weight - relax_weight * value * guess)


def split_dot(value, table):
    rows = value.shape[0]
    high = value.astype(jnp.bfloat16)
    low = (value - high.astype(f32)).astype(jnp.bfloat16)
    both = jnp.dot(jnp.concatenate([high, low], axis=0), table, preferred_element_type=f32)
    return both[:rows] + both[rows:]


def plane_neighbours(plane, below, above):
    rows, lanes = plane.shape
    sub, lane = iota((8, 128), 0), iota((8, 128), 1)
    n_rows, n_lanes = rows // 8, lanes // 128
    tiles = [
        [plane[r * 8:r * 8 + 8, b * 128:b * 128 + 128] for b in range(n_lanes)]
        for r in range(n_rows)]
    lower = [[pltpu.roll(tile, 1, 0) for tile in line] for line in tiles]
    upper = [[pltpu.roll(tile, 7, 0) for tile in line] for line in tiles]
    total = []
    for r in range(n_rows):
        left = [pltpu.roll(tile, 1, 1) for tile in tiles[r]]
        right = [pltpu.roll(tile, 127, 1) for tile in tiles[r]]
        line = []
        for b in range(n_lanes):
            edge = slice(b * 128, b * 128 + 128)
            low = lower[r - 1][b] if r else below[:, edge]
            high = upper[r + 1][b] if r < n_rows - 1 else above[:, edge]
            far_left = left[b - 1] if b else 0.0
            far_right = right[b + 1] if b < n_lanes - 1 else 0.0
            line.append(
                (jnp.where(sub == 0, low, lower[r][b]) + jnp.where(sub == 7, high, upper[r][b]))
                + (jnp.where(lane == 0, far_left, left[b])
                   + jnp.where(lane == 127, far_right, right[b])))
        total.append(jnp.concatenate(line, axis=1) if n_lanes > 1 else line[0])
    return jnp.concatenate(total, axis=0) if n_rows > 1 else total[0]


def kernel(
    n_gx, n_gy, nx, ny, nz,
    rs_hbm, dg_hbm, p0, im0, rs, alpha_ref,
    dg, inv0, g0, q0, ysrc0, ydst0, ysrcq, ydstq,
    pair1, inv1, g1, ysrc1, ydst1, dup1,
    pair2, inv2, g2, ysrc2, ydst2, dup2,
    pair3, gathered, sol, bands, expanded, sums,
    down0, down1, up0, up1, up3,
    load_sem, face_send, face_recv,
    piece_send, piece_recv, line_send, line_recv, peer_send, peer_recv, twin_send, twin_recv,
    sum_send, sum_recv, sum2_send, sum2_recv,
):
    ax, ay = lax.axis_index("gx"), lax.axis_index("gy")
    chunk = 8
    n_chunks = nx // chunk
    nx1, ny1, nz1 = nx // 2, ny // 2, nz // 2
    nx2, ny2, nz2 = nx // 4, ny // 4, nz // 4
    nx3, ny3, nz3 = nx // 8, ny // 8, nz // 8
    half = n_gx // 2

    def load(part, c):
        source, target = ((rs_hbm, rs), (dg_hbm, dg))[part]
        span = pl.ds(c * chunk, chunk)
        return pltpu.make_async_copy(source.at[span], target.at[span], load_sem.at[part, c])

    for c in range(n_chunks):
        load(0, c).start()
        load(1, c).start()

    barrier = pltpu.get_barrier_semaphore()

    def greet_line(k, carry):
        pl.semaphore_signal(barrier, inc=1, device_id=(ax, lax.rem(ay + k, n_gy)), device_id_type=MESH)
        return carry

    def greet_row(k, carry):
        pl.semaphore_signal(barrier, inc=1, device_id=(lax.rem(ax + k, n_gx), ay), device_id_type=MESH)
        return carry

    lax.fori_loop(1, n_gy, greet_line, 0)
    lax.fori_loop(1, n_gx, greet_row, 0)

    def down_table(ref):
        row, column = iota(ref.shape, 0), iota(ref.shape, 1)
        ref[...] = jnp.where((row >> 1) == column, 0.125, 0.0).astype(jnp.bfloat16)

    def up_table(ref, shift):
        row, column = iota(ref.shape, 0), iota(ref.shape, 1)
        ref[...] = jnp.where(row == (column >> shift), 1.0, 0.0).astype(jnp.bfloat16)

    down_table(down0)
    down_table(down1)
    up_table(up0, 1)
    up_table(up1, 1)
    up_table(up3, 3)
    sol[...] = jnp.zeros(sol.shape, f32)

    sides = (
        (ax > 0, (ax - 1, ay)),
        (ax < n_gx - 1, (ax + 1, ay)),
        (ay > 0, (ax, ay - 1)),
        (ay < n_gy - 1, (ax, ay + 1)),
    )

    def faces(group, field, ysrc, ydst, n_sides=4):
        count = ysrc.shape[1]
        pairs = (
            (field.at[1], field.at[count + 1]),
            (field.at[count], field.at[0]),
            (ysrc.at[0], ydst.at[1]),
            (ysrc.at[1], ydst.at[0]),
        )
        copies = []
        for side, (source, target) in enumerate(pairs[:n_sides]):
            there, device = sides[side]
            copies.append((there, pltpu.make_async_remote_copy(
                src_ref=source, dst_ref=target,
                send_sem=face_send.at[group, side], recv_sem=face_recv.at[group, side ^ 1],
                device_id=device, device_id_type=MESH,
            )))
        return copies

    def start_faces(copies):
        for there, copy in copies:
            pl.when(there)(copy.start)

    def clear_faces(field, ydst):
        targets = (field.at[0], field.at[field.shape[0] - 1], ydst.at[0], ydst.at[1])
        for (there, _), target in zip(sides, targets):
            @pl.when(jnp.logical_not(there))
            def _():
                target[...] = jnp.zeros(target.shape, f32)

    def wait_faces(group, field, ysrc, ydst, n_sides=4):
        count = ysrc.shape[1]
        targets = (field.at[0], field.at[count + 1], ydst.at[0], ydst.at[1])
        for side, target in enumerate(targets[:n_sides]):
            there, device = sides[side]
            copy = pltpu.make_async_remote_copy(
                src_ref=target, dst_ref=target,
                send_sem=face_send.at[group, side], recv_sem=face_recv.at[group, side],
                device_id=device, device_id_type=MESH,
            )
            pl.when(there)(copy.wait_recv)

    def piece(group, ysrc, ydst, c, side):
        span = pl.ds(c * chunk, chunk)
        there, device = sides[2 + side]
        return there, pltpu.make_async_remote_copy(
            src_ref=ysrc.at[side, span], dst_ref=ydst.at[1 - side, span],
            send_sem=piece_send.at[group, side, c], recv_sem=piece_recv.at[group, 1 - side, c],
            device_id=device, device_id_type=MESH,
        )

    def start_piece(group, ysrc, ydst, c):
        for side in range(2):
            there, copy = piece(group, ysrc, ydst, c, side)
            pl.when(there)(copy.start)

    def await_piece(group, ysrc, ydst, c):
        for side in range(2):
            span = pl.ds(c * chunk, chunk)
            there, device = sides[2 + side]
            copy = pltpu.make_async_remote_copy(
                src_ref=ysrc.at[side, span], dst_ref=ydst.at[side, span],
                send_sem=piece_send.at[group, side, c], recv_sem=piece_recv.at[group, side, c],
                device_id=device, device_id_type=MESH,
            )
            pl.when(there)(copy.wait_recv)

    for field, ydst in ((g0, ydst0), (g1, ydst1), (g2, ydst2), (q0, ydstq)):
        clear_faces(field, ydst)

    def first_chunk(c):
        load(0, c).wait()
        load(1, c).wait()

        stacked = []
        for k in range(chunk // 2):
            j = c * (chunk // 2) + k
            for i in (2 * j, 2 * j + 1):
                inverse = inverse_of(6.0 + dg[i])
                guess = inverse * rs[i]
                inv0[i] = inverse
                g0[i + 1] = guess
                ysrc0[0, i] = guess[:1]
                ysrc0[1, i] = guess[ny - 1:]
            stacked += [rs[2 * j] + rs[2 * j + 1], dg[2 * j] + dg[2 * j + 1]]
        thin = split_dot(jnp.concatenate(stacked, axis=0), down0[...])
        for k in range(chunk // 2):
            for part in range(2):
                first = (2 * k + part) * ny
                for b in range(nz1 // 128):
                    pair1[part, b, c * (chunk // 2) + k] = thin[first:first + ny, b * 128:(b + 1) * 128]

    def first_step(c, carry):
        first_chunk(c)
        start_piece(0, ysrc0, ydst0, c)
        return carry

    first_chunk(0)
    pl.semaphore_wait(barrier, n_gy + n_gx - 2)
    start_piece(0, ysrc0, ydst0, 0)
    lax.fori_loop(1, n_chunks, first_step, 0)
    copies0 = faces(0, g0, ysrc0, ydst0, 2)
    start_faces(copies0)

    group = min(16, nx1)

    def mid_group(h, carry):
        def halved(part, i):
            return jnp.concatenate([
                pair1[part, b, i, pl.ds(0, ny1, 2), :] + pair1[part, b, i, pl.ds(1, ny1, 2), :]
                for b in range(nz1 // 128)
            ], axis=1)

        stacked = []
        for k in range(group // 2):
            planes = []
            for i in (h * group + 2 * k, h * group + 2 * k + 1):
                res, coef = halved(0, i), halved(1, i)
                inverse = inverse_of(1.5 + coef)
                guess = inverse * res
                inv1[i] = inverse * 0.25
                g1[i + 1] = guess
                ysrc1[0, i] = guess[:1]
                ysrc1[1, i] = guess[ny1 - 1:]
                planes.append((res, coef))
            stacked += [planes[0][0] + planes[1][0], planes[0][1] + planes[1][1]]
        thin = split_dot(jnp.concatenate(stacked, axis=0), down1[...])
        for k in range(group // 2):
            for part in range(2):
                first = (2 * k + part) * ny1
                pair2[part, h * (group // 2) + k] = thin[first:first + ny1]
        return carry

    lax.fori_loop(0, nx1 // group, mid_group, 0)
    copies1 = faces(1, g1, ysrc1, ydst1)
    start_faces(copies1)

    low = []
    for i in range(nx2):
        res, coef = (
            pair2[part, i, pl.ds(0, ny2, 2), :] + pair2[part, i, pl.ds(1, ny2, 2), :]
            for part in range(2))
        inverse = inverse_of(0.375 + coef)
        guess = inverse * res
        inv2[i] = inverse * 0.0625
        g2[i + 1] = guess
        ysrc2[0, i] = guess[:1]
        ysrc2[1, i] = guess[ny2 - 1:]
        low.append((res, coef))
    stacked = [
        jnp.concatenate([low[2 * k][part] + low[2 * k + 1][part] for part in range(2)], axis=1)
        for k in range(nx3)]
    pair3[...] = split_dot(jnp.concatenate(stacked, axis=0), down1[...])
    core, height = ax % 2, ax // 2
    for y in range(ny3):
        gathered[core, height, ay, y] = (
            pair3[pl.ds(2 * y, nx3, ny2), :] + pair3[pl.ds(2 * y + 1, nx3, ny2), :])

    def line_copy(k, slot):
        return pltpu.make_async_remote_copy(
            src_ref=gathered.at[core, height, slot], dst_ref=gathered.at[core, height, slot],
            send_sem=line_send.at[k], recv_sem=line_recv.at[slot],
            device_id=(ax, lax.rem(ay + k, n_gy)), device_id_type=MESH,
        )

    def line_start(k, carry):
        line_copy(k, ay).start()
        return carry

    def line_wait(k, carry):
        line_copy(k, lax.rem(ay + k, n_gy)).wait_recv()
        return carry

    def peer_copy(k, slot):
        return pltpu.make_async_remote_copy(
            src_ref=gathered.at[core, slot], dst_ref=gathered.at[core, slot],
            send_sem=peer_send.at[k], recv_sem=peer_recv.at[slot],
            device_id=(lax.rem(height + k, half) * 2 + core, ay), device_id_type=MESH,
        )

    def twin_copy(slot):
        return pltpu.make_async_remote_copy(
            src_ref=gathered.at[slot], dst_ref=gathered.at[slot],
            send_sem=twin_send.at[0], recv_sem=twin_recv.at[0],
            device_id=(height * 2 + 1 - core, ay), device_id_type=MESH,
        )

    lax.fori_loop(1, n_gy, line_start, 0)
    copies2 = faces(2, g2, ysrc2, ydst2)
    start_faces(copies2)

    wait_faces(0, g0, ysrc0, ydst0, 2)

    def fine_smooth(c, carry):
        await_piece(0, ysrc0, ydst0, c)
        for k in range(chunk):
            i = c * chunk + k
            plane = g0[i + 1]
            total = g0[i] + g0[i + 2] + plane_neighbours(plane, ydst0[0, i], ydst0[1, i])
            q0[i + 1] = (2.0 - relax_weight) * plane + inv0[i] * total
        return carry

    lax.fori_loop(0, n_chunks, fine_smooth, 0)

    lax.fori_loop(1, n_gy, line_wait, 0)
    for k in range(1, half):
        peer_copy(k, height).start()

    wait_faces(2, g2, ysrc2, ydst2)
    for i in range(nx2):
        plane = g2[i + 1]
        total = g2[i] + g2[i + 2] + plane_neighbours(plane, ydst2[0, i], ydst2[1, i])
        smooth = (2.0 - relax_weight) * plane + inv2[i] * total
        dup2[i, pl.ds(0, ny2, 2), :] = smooth
        dup2[i, pl.ds(1, ny2, 2), :] = smooth

    wait_faces(1, g1, ysrc1, ydst1)

    def mid_smooth(h, carry):
        source = dup2[pl.ds(h * (group // 2), group // 2)]
        wide = split_dot(source.reshape(group // 2 * ny1, nz2), up1[...])
        for k in range(group):
            i = h * group + k
            plane = g1[i + 1]
            total = g1[i] + g1[i + 2] + plane_neighbours(plane, ydst1[0, i], ydst1[1, i])
            smooth = (2.0 - relax_weight) * plane + inv1[i] * total
            smooth += wide[k // 2 * ny1:(k // 2 + 1) * ny1]
            for b in range(nz1 // 128):
                part = smooth[:, b * 128:(b + 1) * 128]
                dup1[b, i, pl.ds(0, ny1, 2), :] = part
                dup1[b, i, pl.ds(1, ny1, 2), :] = part
        return carry

    lax.fori_loop(0, nx1 // group, mid_smooth, 0)

    for k in range(1, half):
        peer_copy(k, lax.rem(height + k, half)).wait_recv()
    twin_copy(core).start()

    def carry_up(c, carry):
        span = pl.ds(c * (chunk // 2), chunk // 2)
        source = jnp.concatenate(
            [dup1[b, span].reshape(chunk // 2 * ny, 128) for b in range(nz1 // 128)], axis=1)
        wide = split_dot(source, up0[...])
        for k in range(chunk):
            i = c * chunk + k
            smooth = q0[i + 1] + wide[k // 2 * ny:(k // 2 + 1) * ny]
            q0[i + 1] = smooth
            ysrcq[0, i] = smooth[:1]
            ysrcq[1, i] = smooth[ny - 1:]
        start_piece(1, ysrcq, ydstq, c)
        return carry

    lax.fori_loop(0, n_chunks, carry_up, 0)
    copiesq = faces(3, q0, ysrcq, ydstq, 2)
    start_faces(copiesq)

    twin_copy(1 - core).wait_recv()

    wx3, wy3 = nx3 * n_gx, ny3 * n_gy
    hy3 = wy3 // 2
    lanes = 2 * nz3

    def whole(first):
        return jnp.concatenate([
            gathered[a % 2, a // 2, first:first + n_gy // 2].reshape(hy3, nx3, lanes)
            for a in range(n_gx)
        ], axis=1)

    lower, upper = whole(0), whole(n_gy // 2)
    shape = (hy3, wx3, lanes)
    lane, row, level = iota(shape, 2), iota(shape, 1), iota(shape, 0)
    is_low = lane < nz3
    res3 = jnp.where(is_low, lower, pltpu.roll(upper, nz3, 2))
    coef3 = jnp.where(is_low, pltpu.roll(lower, nz3, 2), upper)
    scale3 = 0.25**3
    inverse3 = relax_weight / (6.0 * scale3 + coef3)
    step3 = inverse3 * scale3
    guess3 = inverse3 * res3
    depth = jnp.where(is_low, lane, lane - nz3)
    no_left, no_right = depth == 0, depth == nz3 - 1
    no_down, no_up = row == 0, row == wx3 - 1
    flat_low = iota((1, wx3, lanes), 2) < nz3

    def coarse_neighbours(field):
        first = jnp.where(flat_low, 0.0, pltpu.roll(field[hy3 - 1:], nz3, 2))
        last = jnp.where(flat_low, pltpu.roll(field[:1], nz3, 2), 0.0)
        total = jnp.concatenate([first, field[:hy3 - 1]], axis=0)
        total += jnp.concatenate([field[1:], last], axis=0)
        total += jnp.where(no_down, 0.0, pltpu.roll(field, 1, 1))
        total += jnp.where(no_up, 0.0, pltpu.roll(field, wx3 - 1, 1))
        total += jnp.where(no_left, 0.0, pltpu.roll(field, 1, 2))
        return total + jnp.where(no_right, 0.0, pltpu.roll(field, lanes - 1, 2))

    jac = guess3
    for _ in range(coarse_sweeps - 1):
        jac = (1.0 - relax_weight) * jac + guess3 + step3 * coarse_neighbours(jac)

    def one(flag):
        return jnp.where(flag, 1.0, 0.0)

    ends = one(no_left) + one(no_right) + one(no_down) + one(no_up)
    ends += one(jnp.logical_and(level == 0, is_low))
    ends += one(jnp.logical_and(level == hy3 - 1, jnp.logical_not(is_low)))
    ones_image = scale3 * ends + coef3
    shift = jnp.sum(res3 - ones_image * jac) / jnp.sum(ones_image)
    jac = jac + shift

    sol[1:hy3 + 1, nx3:nx3 + wx3, :] = jnp.where(is_low, jac, 0.0)
    sol[hy3 + 1:wy3 + 1, nx3:nx3 + wx3, :] = jnp.where(is_low, pltpu.roll(jac, nz3, 2), 0.0)

    near = sol[pl.ds(ay * ny3, ny3 + 2), pl.ds(pl.multiple_of(ax * nx3, nx3), 3 * nx3), :]
    wide = split_dot(near.reshape((ny3 + 2) * 3 * nx3, lanes), up3[...])
    expanded[...] = wide.reshape(ny3 + 2, 3 * nx3, nz)
    for y in range(ny3):
        around = expanded[y + 1]
        own = around[nx3:2 * nx3]
        column = iota(own.shape, 1)
        bands[0, y] = own
        bands[1, y] = (
            2.0 * own
            - jnp.where(column == 0, 0.0, pltpu.roll(own, 1, 1))
            - jnp.where(column == nz - 1, 0.0, pltpu.roll(own, nz - 1, 1)))
        bands[2, y] = own - expanded[y, nx3:2 * nx3]
        bands[3, y] = own - expanded[y + 2, nx3:2 * nx3]
        bands[4, y] = own - pltpu.roll(around, 1, 0)[nx3:2 * nx3]
        bands[5, y] = own - pltpu.roll(around, 3 * nx3 - 1, 0)[nx3:2 * nx3]

    wait_faces(3, q0, ysrcq, ydstq, 2)

    fold = ny // ny3

    def fold_plane(value):
        total = value.reshape(ny // 8, 8, nz).sum(axis=0)
        return sum(total[:, b * 128:(b + 1) * 128] for b in range(nz // 128))

    def last_chunk(c, carry):
        await_piece(1, ysrcq, ydstq, c)

        def rows(kind):
            return [
                jnp.broadcast_to(bands[kind, y, pl.ds(c, 1), :], (fold, nz)) for y in range(ny3)]

        def laid(parts):
            return jnp.concatenate(parts, axis=0)

        sub = iota((fold, nz), 0)
        own = laid(rows(0))
        edge = laid([
            flat + jnp.where(sub == 0, down, 0.0) + jnp.where(sub == fold - 1, up, 0.0)
            for flat, down, up in zip(rows(1), rows(2), rows(3))])
        rz, zq = carry
        for k in range(chunk):
            i = c * chunk + k
            plane = q0[i + 1]
            near_sum = q0[i] + q0[i + 2] + plane_neighbours(plane, ydstq[0, i], ydstq[1, i])
            precond = plane + own
            image = 6.0 * plane - near_sum + dg[i] * precond + edge
            if k == 0:
                image += laid(rows(4))
            if k == chunk - 1:
                image += laid(rows(5))
            p0[i] = precond
            im0[i] = image
            rz += fold_plane(rs[i] * precond)
            zq += fold_plane(precond * image)
        return rz, zq

    zero = jnp.zeros((8, 128), f32)
    rz, zq = lax.fori_loop(0, n_chunks, last_chunk, (zero, zero))

    def sum_copy(k, slot):
        return pltpu.make_async_remote_copy(
            src_ref=sums.at[slot], dst_ref=sums.at[slot],
            send_sem=sum_send.at[k], recv_sem=sum_recv.at[slot],
            device_id=(ax, lax.rem(ay + k, n_gy)), device_id_type=MESH,
        )

    def sum2_copy(k, slot):
        return pltpu.make_async_remote_copy(
            src_ref=sums.at[n_gy + slot], dst_ref=sums.at[n_gy + slot],
            send_sem=sum2_send.at[k], recv_sem=sum2_recv.at[slot],
            device_id=(lax.rem(ax + k, n_gx), ay), device_id_type=MESH,
        )

    sums[ay] = jnp.concatenate(
        [rz.sum(axis=0, keepdims=True), zq.sum(axis=0, keepdims=True)], axis=0)
    for k in range(1, n_gy):
        sum_copy(k, ay).start()
    for k in range(1, n_gy):
        sum_copy(k, lax.rem(ay + k, n_gy)).wait_recv()
    sums[n_gy + ax] = sum(sums[k] for k in range(n_gy))
    for k in range(1, n_gx):
        sum2_copy(k, ax).start()
    for k in range(1, n_gx):
        sum2_copy(k, lax.rem(ax + k, n_gx)).wait_recv()
    total = sum(sums[n_gy + k] for k in range(n_gx))
    both = jnp.sum(total, axis=1, keepdims=True)
    alpha_ref[...] = jnp.broadcast_to(both[:1] / both[1:], alpha_ref.shape)

    for copies in (copies0, copies1, copies2, copiesq):
        for there, copy in copies:
            pl.when(there)(copy.wait_send)

    def pieces_sent(c, carry):
        for group, (ysrc, ydst) in enumerate(((ysrc0, ydst0), (ysrcq, ydstq))):
            for side in range(2):
                there, copy = piece(group, ysrc, ydst, c, side)
                pl.when(there)(copy.wait_send)
        return carry

    lax.fori_loop(0, n_chunks, pieces_sent, 0)

    def line_sent(k, carry):
        line_copy(k, ay).wait_send()
        return carry

    lax.fori_loop(1, n_gy, line_sent, 0)
    for k in range(1, half):
        peer_copy(k, height).wait_send()
    twin_copy(core).wait_send()
    for k in range(1, n_gy):
        sum_copy(k, ay).wait_send()
    for k in range(1, n_gx):
        sum2_copy(k, ax).wait_send()


def scale_kernel(nx, precond, image, right, alpha_ref, update_hbm, residual_hbm, update, residual, sem):
    chunk = 8

    def store(part, c):
        source, target = ((update, update_hbm), (residual, residual_hbm))[part]
        span = pl.ds(c * chunk, chunk)
        return pltpu.make_async_copy(source.at[span], target.at[span], sem.at[part, c])

    alpha = alpha_ref[:1, :1]

    def step(c, carry):
        for k in range(chunk):
            update[c * chunk + k] = alpha * precond[c * chunk + k]
        store(0, c).start()
        for k in range(chunk):
            i = c * chunk + k
            residual[i] = right[i] - alpha * image[i]
        store(1, c).start()
        return carry

    lax.fori_loop(0, nx // chunk, step, 0)

    def finish(c, carry):
        store(0, c).wait()
        store(1, c).wait()
        return carry

    lax.fori_loop(0, nx // chunk, finish, 0)


def body(right_side, diagonal):
    n_gx, n_gy = lax.axis_size("gx"), lax.axis_size("gy")
    nx, ny, nz = right_side.shape
    V = lambda *shape: pltpu.VMEM(shape, f32)
    B = lambda *shape: pltpu.VMEM(shape, jnp.bfloat16)
    D = lambda *shape: pltpu.SemaphoreType.DMA(shape)
    nx1, ny1, nz1 = nx // 2, ny // 2, nz // 2
    nx2, ny2, nz2 = nx // 4, ny // 4, nz // 4
    nx3, ny3, nz3 = nx // 8, ny // 8, nz // 8
    block = V(nx, ny, nz)
    scratch = [
        block, block, V(nx + 2, ny, nz), V(nx + 2, ny, nz),
        V(2, nx, 1, nz), V(2, nx, 1, nz), V(2, nx, 1, nz), V(2, nx, 1, nz),
        V(2, nz1 // 128, nx1, ny, 128), V(nx1, ny1, nz1), V(nx1 + 2, ny1, nz1),
        V(2, nx1, 1, nz1), V(2, nx1, 1, nz1), V(nz1 // 128, nx1, ny, 128),
        V(2, nx2, ny1, nz2), V(nx2, ny2, nz2), V(nx2 + 2, ny2, nz2),
        V(2, nx2, 1, nz2), V(2, nx2, 1, nz2), V(nx2, ny1, nz2),
        V(nx3 * ny2, 2 * nz3), V(2, n_gx // 2, n_gy, ny3, nx3, 2 * nz3),
        V(ny3 * n_gy + 2, nx3 * (n_gx + 2), 2 * nz3), V(6, ny3, nx3, nz), V(ny3 + 2, 3 * nx3, nz),
        V(n_gx + n_gy, 2, 128),
        B(nz, nz1), B(nz1, nz2),
        B(nz1, nz), B(nz2, nz1), B(2 * nz3, nz),
        D(2, nx // 8), D(4, 4), D(4, 4), D(2, 2, nx // 8), D(2, 2, nx // 8),
        D(n_gy), D(n_gy), D(n_gx), D(n_gx), D(1), D(1),
        D(n_gy), D(n_gy), D(n_gx), D(n_gx),
    ]
    precond, image, right, alpha = pl.pallas_call(
        functools.partial(kernel, n_gx, n_gy, nx, ny, nz),
        out_shape=(block, block, block, V(8, 128)),
        in_specs=[pl.BlockSpec(memory_space=pl.ANY)] * 2,
        out_specs=[pl.BlockSpec(memory_space=pltpu.VMEM)] * 4,
        scratch_shapes=scratch,
        compiler_params=pltpu.CompilerParams(
            collective_id=0, has_side_effects=True, vmem_limit_bytes=40 * 1024 * 1024),
        name="cycle",
    )(right_side, diagonal)
    whole = jax.ShapeDtypeStruct(right_side.shape, f32)
    return pl.pallas_call(
        functools.partial(scale_kernel, nx),
        out_shape=(whole, whole),
        in_specs=[pl.BlockSpec(memory_space=pltpu.VMEM)] * 4,
        out_specs=[pl.BlockSpec(memory_space=pl.ANY)] * 2,
        scratch_shapes=[block, block, D(2, nx // 8)],
        compiler_params=pltpu.CompilerParams(vmem_limit_bytes=24 * 1024 * 1024),
        name="scale",
    )(precond, image, right, alpha)


def solution(mesh):
    placed = (P("gx", "gy", None), P("gx", "gy", None))
    return jax.shard_map(
        body,
        mesh=mesh,
        in_specs=placed,
        out_specs=(P("gx", "gy", None), P("gx", "gy", None)),
        check_vma=False,
    )
```

```python
import functools

import jax
import jax.numpy as jnp
from jax import lax
from jax.experimental import pallas as pl
from jax.experimental.pallas import tpu as pltpu
from jax.sharding import PartitionSpec as P

relax_weight = 0.8
coarse_sweeps = 8
MESH = pl.DeviceIdType.MESH
f32 = jnp.float32


def iota(shape, dim):
    return lax.broadcasted_iota(jnp.int32, shape, dim)


def inverse_of(value):
    guess = pl.reciprocal(value, approx=True)
    return guess * (2.0 * relax_weight - relax_weight * value * guess)


def split_dot(value, table):
    rows = value.shape[0]
    high = value.astype(jnp.bfloat16)
    low = (value - high.astype(f32)).astype(jnp.bfloat16)
    both = jnp.dot(jnp.concatenate([high, low], axis=0), table, preferred_element_type=f32)
    return both[:rows] + both[rows:]


def plane_neighbours(plane, below, above):
    rows, lanes = plane.shape
    sub, lane = iota((8, 128), 0), iota((8, 128), 1)
    n_rows, n_lanes = rows // 8, lanes // 128
    tiles = [
        [plane[r * 8:r * 8 + 8, b * 128:b * 128 + 128] for b in range(n_lanes)]
        for r in range(n_rows)]
    lower = [[pltpu.roll(tile, 1, 0) for tile in line] for line in tiles]
    upper = [[pltpu.roll(tile, 7, 0) for tile in line] for line in tiles]
    total = []
    for r in range(n_rows):
        left = [pltpu.roll(tile, 1, 1) for tile in tiles[r]]
        right = [pltpu.roll(tile, 127, 1) for tile in tiles[r]]
        line = []
        for b in range(n_lanes):
            edge = slice(b * 128, b * 128 + 128)
            low = lower[r - 1][b] if r else below[:, edge]
            high = upper[r + 1][b] if r < n_rows - 1 else above[:, edge]
            far_left = left[b - 1] if b else 0.0
            far_right = right[b + 1] if b < n_lanes - 1 else 0.0
            line.append(
                (jnp.where(sub == 0, low, lower[r][b]) + jnp.where(sub == 7, high, upper[r][b]))
                + (jnp.where(lane == 0, far_left, left[b])
                   + jnp.where(lane == 127, far_right, right[b])))
        total.append(jnp.concatenate(line, axis=1) if n_lanes > 1 else line[0])
    return jnp.concatenate(total, axis=0) if n_rows > 1 else total[0]


def kernel(
    n_gx, n_gy, nx, ny, nz,
    rs_hbm, dg_hbm, p0, im0, rs, alpha_ref,
    dg, inv0, g0, q0, ysrc0, ydst0, ysrcq, ydstq,
    pair1, inv1, g1, ysrc1, ydst1, dup1,
    pair2, inv2, g2, ysrc2, ydst2, dup2,
    pair3, gathered, sol, bands, expanded, sums,
    down0, down1, up0, up1, up3,
    load_sem, face_send, face_recv,
    piece_send, piece_recv, line_send, line_recv, twin_send, twin_recv, sum_send, sum_recv,
):
    ax, ay = lax.axis_index("gx"), lax.axis_index("gy")
    chunk = 8
    n_chunks = nx // chunk
    nx1, ny1, nz1 = nx // 2, ny // 2, nz // 2
    nx2, ny2, nz2 = nx // 4, ny // 4, nz // 4
    nx3, ny3, nz3 = nx // 8, ny // 8, nz // 8
    n_all = n_gx * n_gy
    n_same = n_all // 2
    core, me = ax % 2, ax * n_gy + ay
    place = ax // 2 * n_gy + ay

    def load(part, c):
        source, target = ((rs_hbm, rs), (dg_hbm, dg))[part]
        span = pl.ds(c * chunk, chunk)
        return pltpu.make_async_copy(source.at[span], target.at[span], load_sem.at[part, c])

    for c in range(n_chunks):
        load(0, c).start()
        load(1, c).start()

    barrier = pltpu.get_barrier_semaphore()

    def other(k):
        device = lax.rem(me + k, n_all)
        return (device // n_gy, device % n_gy)

    def greet(k, carry):
        pl.semaphore_signal(barrier, inc=1, device_id=other(k), device_id_type=MESH)
        return carry

    lax.fori_loop(1, n_all, greet, 0)

    def down_table(ref):
        row, column = iota(ref.shape, 0), iota(ref.shape, 1)
        ref[...] = jnp.where((row >> 1) == column, 0.125, 0.0).astype(jnp.bfloat16)

    def up_table(ref, shift):
        row, column = iota(ref.shape, 0), iota(ref.shape, 1)
        ref[...] = jnp.where(row == (column >> shift), 1.0, 0.0).astype(jnp.bfloat16)

    down_table(down0)
    down_table(down1)
    up_table(up0, 1)
    up_table(up1, 1)
    up_table(up3, 3)
    sol[...] = jnp.zeros(sol.shape, f32)

    sides = (
        (ax > 0, (ax - 1, ay)),
        (ax < n_gx - 1, (ax + 1, ay)),
        (ay > 0, (ax, ay - 1)),
        (ay < n_gy - 1, (ax, ay + 1)),
    )

    def faces(group, field, ysrc, ydst, n_sides=4):
        count = ysrc.shape[1]
        pairs = (
            (field.at[1], field.at[count + 1]),
            (field.at[count], field.at[0]),
            (ysrc.at[0], ydst.at[1]),
            (ysrc.at[1], ydst.at[0]),
        )
        copies = []
        for side, (source, target) in enumerate(pairs[:n_sides]):
            there, device = sides[side]
            copies.append((there, pltpu.make_async_remote_copy(
                src_ref=source, dst_ref=target,
                send_sem=face_send.at[group, side], recv_sem=face_recv.at[group, side ^ 1],
                device_id=device, device_id_type=MESH,
            )))
        return copies

    def start_faces(copies):
        for there, copy in copies:
            pl.when(there)(copy.start)

    def clear_faces(field, ydst):
        targets = (field.at[0], field.at[field.shape[0] - 1], ydst.at[0], ydst.at[1])
        for (there, _), target in zip(sides, targets):
            @pl.when(jnp.logical_not(there))
            def _():
                target[...] = jnp.zeros(target.shape, f32)

    def wait_faces(group, field, ysrc, ydst, n_sides=4):
        count = ysrc.shape[1]
        targets = (field.at[0], field.at[count + 1], ydst.at[0], ydst.at[1])
        for side, target in enumerate(targets[:n_sides]):
            there, device = sides[side]
            copy = pltpu.make_async_remote_copy(
                src_ref=target, dst_ref=target,
                send_sem=face_send.at[group, side], recv_sem=face_recv.at[group, side],
                device_id=device, device_id_type=MESH,
            )
            pl.when(there)(copy.wait_recv)

    def piece(group, ysrc, ydst, c, side):
        span = pl.ds(c * chunk, chunk)
        there, device = sides[2 + side]
        return there, pltpu.make_async_remote_copy(
            src_ref=ysrc.at[side, span], dst_ref=ydst.at[1 - side, span],
            send_sem=piece_send.at[group, side, c], recv_sem=piece_recv.at[group, 1 - side, c],
            device_id=device, device_id_type=MESH,
        )

    def start_piece(group, ysrc, ydst, c):
        for side in range(2):
            there, copy = piece(group, ysrc, ydst, c, side)
            pl.when(there)(copy.start)

    def await_piece(group, ysrc, ydst, c):
        for side in range(2):
            span = pl.ds(c * chunk, chunk)
            there, device = sides[2 + side]
            copy = pltpu.make_async_remote_copy(
                src_ref=ysrc.at[side, span], dst_ref=ydst.at[side, span],
                send_sem=piece_send.at[group, side, c], recv_sem=piece_recv.at[group, side, c],
                device_id=device, device_id_type=MESH,
            )
            pl.when(there)(copy.wait_recv)

    for field, ydst in ((g0, ydst0), (g1, ydst1), (g2, ydst2), (q0, ydstq)):
        clear_faces(field, ydst)

    def first_chunk(c):
        load(0, c).wait()
        load(1, c).wait()

        stacked = []
        for k in range(chunk // 2):
            j = c * (chunk // 2) + k
            for i in (2 * j, 2 * j + 1):
                inverse = inverse_of(6.0 + dg[i])
                guess = inverse * rs[i]
                inv0[i] = inverse
                g0[i + 1] = guess
                ysrc0[0, i] = guess[:1]
                ysrc0[1, i] = guess[ny - 1:]
            stacked += [rs[2 * j] + rs[2 * j + 1], dg[2 * j] + dg[2 * j + 1]]
        thin = split_dot(jnp.concatenate(stacked, axis=0), down0[...])
        for k in range(chunk // 2):
            for part in range(2):
                first = (2 * k + part) * ny
                for b in range(nz1 // 128):
                    pair1[part, b, c * (chunk // 2) + k] = thin[first:first + ny, b * 128:(b + 1) * 128]

    def first_step(c, carry):
        first_chunk(c)
        start_piece(0, ysrc0, ydst0, c)
        return carry

    first_chunk(0)
    pl.semaphore_wait(barrier, n_all - 1)
    start_piece(0, ysrc0, ydst0, 0)
    lax.fori_loop(1, n_chunks, first_step, 0)
    copies0 = faces(0, g0, ysrc0, ydst0, 2)
    start_faces(copies0)

    group = min(16, nx1)

    def mid_group(h, carry):
        def halved(part, i):
            return jnp.concatenate([
                pair1[part, b, i, pl.ds(0, ny1, 2), :] + pair1[part, b, i, pl.ds(1, ny1, 2), :]
                for b in range(nz1 // 128)
            ], axis=1)

        stacked = []
        for k in range(group // 2):
            planes = []
            for i in (h * group + 2 * k, h * group + 2 * k + 1):
                res, coef = halved(0, i), halved(1, i)
                inverse = inverse_of(1.5 + coef)
                guess = inverse * res
                inv1[i] = inverse * 0.25
                g1[i + 1] = guess
                ysrc1[0, i] = guess[:1]
                ysrc1[1, i] = guess[ny1 - 1:]
                planes.append((res, coef))
            stacked += [planes[0][0] + planes[1][0], planes[0][1] + planes[1][1]]
        thin = split_dot(jnp.concatenate(stacked, axis=0), down1[...])
        for k in range(group // 2):
            for part in range(2):
                first = (2 * k + part) * ny1
                pair2[part, h * (group // 2) + k] = thin[first:first + ny1]
        return carry

    lax.fori_loop(0, nx1 // group, mid_group, 0)
    copies1 = faces(1, g1, ysrc1, ydst1)
    start_faces(copies1)

    low = []
    for i in range(nx2):
        res, coef = (
            pair2[part, i, pl.ds(0, ny2, 2), :] + pair2[part, i, pl.ds(1, ny2, 2), :]
            for part in range(2))
        inverse = inverse_of(0.375 + coef)
        guess = inverse * res
        inv2[i] = inverse * 0.0625
        g2[i + 1] = guess
        ysrc2[0, i] = guess[:1]
        ysrc2[1, i] = guess[ny2 - 1:]
        low.append((res, coef))
    stacked = [
        jnp.concatenate([low[2 * k][part] + low[2 * k + 1][part] for part in range(2)], axis=1)
        for k in range(nx3)]
    pair3[...] = split_dot(jnp.concatenate(stacked, axis=0), down1[...])
    for y in range(ny3):
        gathered[core, place, y] = (
            pair3[pl.ds(2 * y, nx3, ny2), :] + pair3[pl.ds(2 * y + 1, nx3, ny2), :])

    def line_copy(k, slot):
        target = lax.rem(place + k, n_same)
        return pltpu.make_async_remote_copy(
            src_ref=gathered.at[core, slot], dst_ref=gathered.at[core, slot],
            send_sem=line_send.at[k], recv_sem=line_recv.at[slot],
            device_id=(target // n_gy * 2 + core, target % n_gy), device_id_type=MESH,
        )

    def line_start(k, carry):
        line_copy(k, place).start()
        return carry

    def line_wait(k, carry):
        line_copy(k, lax.rem(place + k, n_same)).wait_recv()
        return carry

    def twin_copy(slot):
        return pltpu.make_async_remote_copy(
            src_ref=gathered.at[slot], dst_ref=gathered.at[slot],
            send_sem=twin_send.at[0], recv_sem=twin_recv.at[0],
            device_id=(ax + 1 - 2 * core, ay), device_id_type=MESH,
        )

    lax.fori_loop(1, n_same, line_start, 0)
    copies2 = faces(2, g2, ysrc2, ydst2)
    start_faces(copies2)

    wait_faces(0, g0, ysrc0, ydst0, 2)

    def fine_smooth(c, carry):
        await_piece(0, ysrc0, ydst0, c)
        for k in range(chunk):
            i = c * chunk + k
            plane = g0[i + 1]
            total = g0[i] + g0[i + 2] + plane_neighbours(plane, ydst0[0, i], ydst0[1, i])
            q0[i + 1] = (2.0 - relax_weight) * plane + inv0[i] * total
        return carry

    lax.fori_loop(0, n_chunks, fine_smooth, 0)

    wait_faces(2, g2, ysrc2, ydst2)
    for i in range(nx2):
        plane = g2[i + 1]
        total = g2[i] + g2[i + 2] + plane_neighbours(plane, ydst2[0, i], ydst2[1, i])
        smooth = (2.0 - relax_weight) * plane + inv2[i] * total
        dup2[i, pl.ds(0, ny2, 2), :] = smooth
        dup2[i, pl.ds(1, ny2, 2), :] = smooth

    wait_faces(1, g1, ysrc1, ydst1)

    def mid_smooth(h, carry):
        source = dup2[pl.ds(h * (group // 2), group // 2)]
        wide = split_dot(source.reshape(group // 2 * ny1, nz2), up1[...])
        for k in range(group):
            i = h * group + k
            plane = g1[i + 1]
            total = g1[i] + g1[i + 2] + plane_neighbours(plane, ydst1[0, i], ydst1[1, i])
            smooth = (2.0 - relax_weight) * plane + inv1[i] * total
            smooth += wide[k // 2 * ny1:(k // 2 + 1) * ny1]
            for b in range(nz1 // 128):
                part = smooth[:, b * 128:(b + 1) * 128]
                dup1[b, i, pl.ds(0, ny1, 2), :] = part
                dup1[b, i, pl.ds(1, ny1, 2), :] = part
        return carry

    lax.fori_loop(0, nx1 // group, mid_smooth, 0)

    lax.fori_loop(1, n_same, line_wait, 0)
    twin_copy(core).start()

    step_chunks = 2 if n_chunks % 2 == 0 else 1
    step = step_chunks * chunk

    def carry_up(c, carry):
        span = pl.ds(c * (step // 2), step // 2)
        source = jnp.concatenate(
            [dup1[b, span].reshape(step // 2 * ny, 128) for b in range(nz1 // 128)], axis=1)
        wide = split_dot(source, up0[...])
        for k in range(step):
            i = c * step + k
            smooth = q0[i + 1] + wide[k // 2 * ny:(k // 2 + 1) * ny]
            q0[i + 1] = smooth
            ysrcq[0, i] = smooth[:1]
            ysrcq[1, i] = smooth[ny - 1:]
        for k in range(step_chunks):
            start_piece(1, ysrcq, ydstq, c * step_chunks + k)
        return carry

    lax.fori_loop(0, n_chunks // step_chunks, carry_up, 0)
    copiesq = faces(3, q0, ysrcq, ydstq, 2)
    start_faces(copiesq)

    twin_copy(1 - core).wait_recv()

    wx3, wy3 = nx3 * n_gx, ny3 * n_gy
    hy3 = wy3 // 2
    lanes = 2 * nz3

    def whole(first):
        return jnp.concatenate([
            gathered[a % 2, a // 2 * n_gy + first:a // 2 * n_gy + first + n_gy // 2]
            .reshape(hy3, nx3, lanes) for a in range(n_gx)
        ], axis=1)

    lower, upper = whole(0), whole(n_gy // 2)
    shape = (hy3, wx3, lanes)
    lane, row, level = iota(shape, 2), iota(shape, 1), iota(shape, 0)
    is_low = lane < nz3
    res3 = jnp.where(is_low, lower, pltpu.roll(upper, nz3, 2))
    coef3 = jnp.where(is_low, pltpu.roll(lower, nz3, 2), upper)
    scale3 = 0.25**3
    inverse3 = relax_weight / (6.0 * scale3 + coef3)
    step3 = inverse3 * scale3
    guess3 = inverse3 * res3
    depth = jnp.where(is_low, lane, lane - nz3)
    no_left, no_right = depth == 0, depth == nz3 - 1
    no_down, no_up = row == 0, row == wx3 - 1
    flat_low = iota((1, wx3, lanes), 2) < nz3

    def coarse_neighbours(field):
        first = jnp.where(flat_low, 0.0, pltpu.roll(field[hy3 - 1:], nz3, 2))
        last = jnp.where(flat_low, pltpu.roll(field[:1], nz3, 2), 0.0)
        total = jnp.concatenate([first, field[:hy3 - 1]], axis=0)
        total += jnp.concatenate([field[1:], last], axis=0)
        total += jnp.where(no_down, 0.0, pltpu.roll(field, 1, 1))
        total += jnp.where(no_up, 0.0, pltpu.roll(field, wx3 - 1, 1))
        total += jnp.where(no_left, 0.0, pltpu.roll(field, 1, 2))
        return total + jnp.where(no_right, 0.0, pltpu.roll(field, lanes - 1, 2))

    jac = guess3
    for _ in range(coarse_sweeps - 1):
        jac = (1.0 - relax_weight) * jac + guess3 + step3 * coarse_neighbours(jac)

    def one(flag):
        return jnp.where(flag, 1.0, 0.0)

    ends = one(no_left) + one(no_right) + one(no_down) + one(no_up)
    ends += one(jnp.logical_and(level == 0, is_low))
    ends += one(jnp.logical_and(level == hy3 - 1, jnp.logical_not(is_low)))
    ones_image = scale3 * ends + coef3
    shift = jnp.sum(res3 - ones_image * jac) / jnp.sum(ones_image)
    jac = jac + shift

    sol[1:hy3 + 1, nx3:nx3 + wx3, :] = jnp.where(is_low, jac, 0.0)
    sol[hy3 + 1:wy3 + 1, nx3:nx3 + wx3, :] = jnp.where(is_low, pltpu.roll(jac, nz3, 2), 0.0)

    near = sol[pl.ds(ay * ny3, ny3 + 2), pl.ds(pl.multiple_of(ax * nx3, nx3), 3 * nx3), :]
    wide = split_dot(near.reshape((ny3 + 2) * 3 * nx3, lanes), up3[...])
    expanded[...] = wide.reshape(ny3 + 2, 3 * nx3, nz)
    for y in range(ny3):
        around = expanded[y + 1]
        own = around[nx3:2 * nx3]
        column = iota(own.shape, 1)
        bands[0, y] = own
        bands[1, y] = (
            2.0 * own
            - jnp.where(column == 0, 0.0, pltpu.roll(own, 1, 1))
            - jnp.where(column == nz - 1, 0.0, pltpu.roll(own, nz - 1, 1)))
        bands[2, y] = own - expanded[y, nx3:2 * nx3]
        bands[3, y] = own - expanded[y + 2, nx3:2 * nx3]
        bands[4, y] = own - pltpu.roll(around, 1, 0)[nx3:2 * nx3]
        bands[5, y] = own - pltpu.roll(around, 3 * nx3 - 1, 0)[nx3:2 * nx3]

    wait_faces(3, q0, ysrcq, ydstq, 2)

    fold = ny // ny3

    def fold_plane(value):
        total = value.reshape(ny // 8, 8, nz).sum(axis=0)
        return sum(total[:, b * 128:(b + 1) * 128] for b in range(nz // 128))

    def last_chunk(c, carry):
        await_piece(1, ysrcq, ydstq, c)

        def rows(kind):
            return [
                jnp.broadcast_to(bands[kind, y, pl.ds(c, 1), :], (fold, nz)) for y in range(ny3)]

        def laid(parts):
            return jnp.concatenate(parts, axis=0)

        sub = iota((fold, nz), 0)
        own = laid(rows(0))
        edge = laid([
            flat + jnp.where(sub == 0, down, 0.0) + jnp.where(sub == fold - 1, up, 0.0)
            for flat, down, up in zip(rows(1), rows(2), rows(3))])
        rz, zq = carry
        for k in range(chunk):
            i = c * chunk + k
            plane = q0[i + 1]
            near_sum = q0[i] + q0[i + 2] + plane_neighbours(plane, ydstq[0, i], ydstq[1, i])
            precond = plane + own
            image = 6.0 * plane - near_sum + dg[i] * precond + edge
            if k == 0:
                image += laid(rows(4))
            if k == chunk - 1:
                image += laid(rows(5))
            p0[i] = precond
            im0[i] = image
            rz += fold_plane(rs[i] * precond)
            zq += fold_plane(precond * image)
        return rz, zq

    zero = jnp.zeros((8, 128), f32)
    rz, zq = lax.fori_loop(0, n_chunks, last_chunk, (zero, zero))

    def sum_copy(k, slot):
        return pltpu.make_async_remote_copy(
            src_ref=sums.at[slot], dst_ref=sums.at[slot],
            send_sem=sum_send.at[k], recv_sem=sum_recv.at[slot],
            device_id=other(k), device_id_type=MESH,
        )

    def sum_start(k, carry):
        sum_copy(k, me).start()
        return carry

    def sum_wait(k, carry):
        sum_copy(k, lax.rem(me + k, n_all)).wait_recv()
        return carry

    sums[me] = jnp.concatenate(
        [rz.sum(axis=0, keepdims=True), zq.sum(axis=0, keepdims=True)], axis=0)
    lax.fori_loop(1, n_all, sum_start, 0)
    lax.fori_loop(1, n_all, sum_wait, 0)
    total = sum(sums[k] for k in range(n_all))
    both = jnp.sum(total, axis=1, keepdims=True)
    alpha_ref[...] = jnp.broadcast_to(both[:1] / both[1:], alpha_ref.shape)

    for copies in (copies0, copies1, copies2, copiesq):
        for there, copy in copies:
            pl.when(there)(copy.wait_send)

    def pieces_sent(c, carry):
        for group, (ysrc, ydst) in enumerate(((ysrc0, ydst0), (ysrcq, ydstq))):
            for side in range(2):
                there, copy = piece(group, ysrc, ydst, c, side)
                pl.when(there)(copy.wait_send)
        return carry

    lax.fori_loop(0, n_chunks, pieces_sent, 0)

    def line_sent(k, carry):
        line_copy(k, place).wait_send()
        return carry

    def sum_sent(k, carry):
        sum_copy(k, me).wait_send()
        return carry

    lax.fori_loop(1, n_same, line_sent, 0)
    twin_copy(core).wait_send()
    lax.fori_loop(1, n_all, sum_sent, 0)


def scale_kernel(nx, precond, image, right, alpha_ref, update_hbm, residual_hbm, update, residual, sem):
    chunk = 8

    def store(part, c):
        source, target = ((update, update_hbm), (residual, residual_hbm))[part]
        span = pl.ds(c * chunk, chunk)
        return pltpu.make_async_copy(source.at[span], target.at[span], sem.at[part, c])

    alpha = alpha_ref[:1, :1]

    def step(c, carry):
        for k in range(chunk):
            update[c * chunk + k] = alpha * precond[c * chunk + k]
        store(0, c).start()
        for k in range(chunk):
            i = c * chunk + k
            residual[i] = right[i] - alpha * image[i]
        store(1, c).start()
        return carry

    lax.fori_loop(0, nx // chunk, step, 0)

    def finish(c, carry):
        store(0, c).wait()
        store(1, c).wait()
        return carry

    lax.fori_loop(0, nx // chunk, finish, 0)


def body(right_side, diagonal):
    n_gx, n_gy = lax.axis_size("gx"), lax.axis_size("gy")
    nx, ny, nz = right_side.shape
    V = lambda *shape: pltpu.VMEM(shape, f32)
    B = lambda *shape: pltpu.VMEM(shape, jnp.bfloat16)
    D = lambda *shape: pltpu.SemaphoreType.DMA(shape)
    nx1, ny1, nz1 = nx // 2, ny // 2, nz // 2
    nx2, ny2, nz2 = nx // 4, ny // 4, nz // 4
    nx3, ny3, nz3 = nx // 8, ny // 8, nz // 8
    block = V(nx, ny, nz)
    scratch = [
        block, block, V(nx + 2, ny, nz), V(nx + 2, ny, nz),
        V(2, nx, 1, nz), V(2, nx, 1, nz), V(2, nx, 1, nz), V(2, nx, 1, nz),
        V(2, nz1 // 128, nx1, ny, 128), V(nx1, ny1, nz1), V(nx1 + 2, ny1, nz1),
        V(2, nx1, 1, nz1), V(2, nx1, 1, nz1), V(nz1 // 128, nx1, ny, 128),
        V(2, nx2, ny1, nz2), V(nx2, ny2, nz2), V(nx2 + 2, ny2, nz2),
        V(2, nx2, 1, nz2), V(2, nx2, 1, nz2), V(nx2, ny1, nz2),
        V(nx3 * ny2, 2 * nz3), V(2, n_gx // 2 * n_gy, ny3, nx3, 2 * nz3),
        V(ny3 * n_gy + 2, nx3 * (n_gx + 2), 2 * nz3), V(6, ny3, nx3, nz), V(ny3 + 2, 3 * nx3, nz),
        V(n_gx * n_gy, 2, 128),
        B(nz, nz1), B(nz1, nz2),
        B(nz1, nz), B(nz2, nz1), B(2 * nz3, nz),
        D(2, nx // 8), D(4, 4), D(4, 4), D(2, 2, nx // 8), D(2, 2, nx // 8),
        D(n_gx * n_gy), D(n_gx * n_gy), D(1), D(1), D(n_gx * n_gy), D(n_gx * n_gy),
    ]
    precond, image, right, alpha = pl.pallas_call(
        functools.partial(kernel, n_gx, n_gy, nx, ny, nz),
        out_shape=(block, block, block, V(8, 128)),
        in_specs=[pl.BlockSpec(memory_space=pl.ANY)] * 2,
        out_specs=[pl.BlockSpec(memory_space=pltpu.VMEM)] * 4,
        scratch_shapes=scratch,
        compiler_params=pltpu.CompilerParams(
            collective_id=0, has_side_effects=True, vmem_limit_bytes=40 * 1024 * 1024),
        name="cycle",
    )(right_side, diagonal)
    whole = jax.ShapeDtypeStruct(right_side.shape, f32)
    return pl.pallas_call(
        functools.partial(scale_kernel, nx),
        out_shape=(whole, whole),
        in_specs=[pl.BlockSpec(memory_space=pltpu.VMEM)] * 4,
        out_specs=[pl.BlockSpec(memory_space=pl.ANY)] * 2,
        scratch_shapes=[block, block, D(2, nx // 8)],
        compiler_params=pltpu.CompilerParams(vmem_limit_bytes=24 * 1024 * 1024),
        name="scale",
    )(precond, image, right, alpha)


def solution(mesh):
    placed = (P("gx", "gy", None), P("gx", "gy", None))
    return jax.shard_map(
        body,
        mesh=mesh,
        in_specs=placed,
        out_specs=(P("gx", "gy", None), P("gx", "gy", None)),
        check_vma=False,
    )
```

```python
import functools

import jax
import jax.numpy as jnp
from jax import lax
from jax.experimental import pallas as pl
from jax.experimental.pallas import tpu as pltpu
from jax.sharding import PartitionSpec as P

relax_weight = 0.8
coarse_sweeps = 8
MESH = pl.DeviceIdType.MESH
f32 = jnp.float32


def iota(shape, dim):
    return lax.broadcasted_iota(jnp.int32, shape, dim)


def inverse_of(value):
    guess = pl.reciprocal(value, approx=True)
    return guess * (2.0 * relax_weight - relax_weight * value * guess)


def split(value):
    high = value.astype(jnp.bfloat16)
    return high, (value - high.astype(f32)).astype(jnp.bfloat16)


def joined_dot(parts, table):
    rows = sum(high.shape[0] for high, _ in parts)
    stacked = [high for high, _ in parts] + [low for _, low in parts]
    both = jnp.dot(jnp.concatenate(stacked, axis=0), table, preferred_element_type=f32)
    return both[:rows] + both[rows:]


def split_dot(value, table):
    return joined_dot([split(value)], table)


def band(r):
    return slice(r * 8, r * 8 + 8)


def band_neighbours(plane, r, below, above, seam=0):
    rows, lanes = plane.shape
    sub, lane = iota((8, 128), 0), iota((8, 128), 1)
    first, last = lane == 0, lane == 127
    if seam:
        first = jnp.logical_or(first, lane == seam)
        last = jnp.logical_or(last, lane == seam - 1)
    centre = plane[band(r), :]
    low = plane[band(r - 1), :] if r else below
    high = plane[band(r + 1), :] if r < rows // 8 - 1 else above
    n_lanes = lanes // 128
    tiles = [centre[:, b * 128:b * 128 + 128] for b in range(n_lanes)]
    line = []
    for b, tile in enumerate(tiles):
        edge = slice(b * 128, b * 128 + 128)
        left = tiles[b - 1] if b else 0.0
        right = tiles[b + 1] if b < n_lanes - 1 else 0.0
        if seam:
            across = jnp.where(first, 0.0, pltpu.roll(tile, 1, 1))
            across += jnp.where(last, 0.0, pltpu.roll(tile, 127, 1))
        else:
            across = pltpu.roll(jnp.where(last, left, tile), 1, 1)
            across += pltpu.roll(jnp.where(first, right, tile), 127, 1)
        along = pltpu.roll(jnp.where(sub == 7, 0.0 if low is None else low[:, edge], tile), 1, 0)
        along += pltpu.roll(jnp.where(sub == 0, 0.0 if high is None else high[:, edge], tile), 7, 0)
        line.append(across + along)
    return centre, jnp.concatenate(line, axis=1) if n_lanes > 1 else line[0]


def smooth_band(field, inverse, ydst, i, r):
    centre, total = band_neighbours(field.at[i + 1], r, ydst[0, i], ydst[1, i])
    total += field[i, band(r), :] + field[i + 2, band(r), :]
    return (2.0 - relax_weight) * centre + inverse[i, band(r), :] * total


def kernel(
    n_gx, n_gy, nx, ny, nz,
    rs_hbm, dg_hbm, p0, im0, rs, alpha_ref,
    dg, inv0, g0, q0, ysrc0, ydst0, ysrcq, ydstq,
    pair1, inv1, g1, ysrc1, ydst1, dup1,
    pair2, inv2, g2, ysrc2, ydst2, dup2,
    pair3, gathered, sol, bands, expanded, sums, step_ref, guess_ref, ones_ref, jac_ref,
    down0, down1, up0, up1, up3,
    load_sem, face_send, face_recv,
    piece_send, piece_recv, line_send, line_recv, twin_send, twin_recv, sum_send, sum_recv,
):
    ax, ay = lax.axis_index("gx"), lax.axis_index("gy")
    chunk = 8
    n_chunks = nx // chunk
    nx1, ny1, nz1 = nx // 2, ny // 2, nz // 2
    nx2, ny2, nz2 = nx // 4, ny // 4, nz // 4
    nx3, ny3, nz3 = nx // 8, ny // 8, nz // 8
    n_all = n_gx * n_gy
    n_same = n_all // 2
    core, me = ax % 2, ax * n_gy + ay
    place = ax // 2 * n_gy + ay

    def load(part, c):
        source, target = ((rs_hbm, rs), (dg_hbm, dg))[part]
        span = pl.ds(c * chunk, chunk)
        return pltpu.make_async_copy(source.at[span], target.at[span], load_sem.at[part, c])

    for c in range(n_chunks):
        load(0, c).start()
        load(1, c).start()

    barrier = pltpu.get_barrier_semaphore()

    def other(k):
        device = lax.rem(me + k, n_all)
        return (device // n_gy, device % n_gy)

    def greet(k, carry):
        pl.semaphore_signal(barrier, inc=1, device_id=other(k), device_id_type=MESH)
        return carry

    lax.fori_loop(1, n_all, greet, 0)

    def down_table(ref):
        row, column = iota(ref.shape, 0), iota(ref.shape, 1)
        ref[...] = jnp.where((row >> 1) == column, 0.125, 0.0).astype(jnp.bfloat16)

    def up_table(ref, shift):
        row, column = iota(ref.shape, 0), iota(ref.shape, 1)
        ref[...] = jnp.where(row == (column >> shift), 1.0, 0.0).astype(jnp.bfloat16)

    down_table(down0)
    down_table(down1)
    up_table(up0, 1)
    up_table(up1, 1)
    up_table(up3, 3)
    sol[...] = jnp.zeros(sol.shape, f32)

    sides = (
        (ax > 0, (ax - 1, ay)),
        (ax < n_gx - 1, (ax + 1, ay)),
        (ay > 0, (ax, ay - 1)),
        (ay < n_gy - 1, (ax, ay + 1)),
    )

    def faces(group, field, ysrc, ydst, n_sides=4):
        count = ysrc.shape[1]
        pairs = (
            (field.at[1], field.at[count + 1]),
            (field.at[count], field.at[0]),
            (ysrc.at[0], ydst.at[1]),
            (ysrc.at[1], ydst.at[0]),
        )
        copies = []
        for side, (source, target) in enumerate(pairs[:n_sides]):
            there, device = sides[side]
            copies.append((there, pltpu.make_async_remote_copy(
                src_ref=source, dst_ref=target,
                send_sem=face_send.at[group, side], recv_sem=face_recv.at[group, side ^ 1],
                device_id=device, device_id_type=MESH,
            )))
        return copies

    def start_faces(copies):
        for there, copy in copies:
            pl.when(there)(copy.start)

    def clear_faces(field, ydst):
        targets = (field.at[0], field.at[field.shape[0] - 1], ydst.at[0], ydst.at[1])
        for (there, _), target in zip(sides, targets):
            @pl.when(jnp.logical_not(there))
            def _():
                target[...] = jnp.zeros(target.shape, f32)

    def wait_faces(group, field, ysrc, ydst, n_sides=4):
        count = ysrc.shape[1]
        targets = (field.at[0], field.at[count + 1], ydst.at[0], ydst.at[1])
        for side, target in enumerate(targets[:n_sides]):
            there, device = sides[side]
            copy = pltpu.make_async_remote_copy(
                src_ref=target, dst_ref=target,
                send_sem=face_send.at[group, side], recv_sem=face_recv.at[group, side],
                device_id=device, device_id_type=MESH,
            )
            pl.when(there)(copy.wait_recv)

    def piece(group, ysrc, ydst, c, side):
        span = pl.ds(c * chunk, chunk)
        there, device = sides[2 + side]
        return there, pltpu.make_async_remote_copy(
            src_ref=ysrc.at[side, span], dst_ref=ydst.at[1 - side, span],
            send_sem=piece_send.at[group, side, c], recv_sem=piece_recv.at[group, 1 - side, c],
            device_id=device, device_id_type=MESH,
        )

    def start_piece(group, ysrc, ydst, c):
        for side in range(2):
            there, copy = piece(group, ysrc, ydst, c, side)
            pl.when(there)(copy.start)

    def await_piece(group, ysrc, ydst, c):
        for side in range(2):
            span = pl.ds(c * chunk, chunk)
            there, device = sides[2 + side]
            copy = pltpu.make_async_remote_copy(
                src_ref=ysrc.at[side, span], dst_ref=ydst.at[side, span],
                send_sem=piece_send.at[group, side, c], recv_sem=piece_recv.at[group, side, c],
                device_id=device, device_id_type=MESH,
            )
            pl.when(there)(copy.wait_recv)

    for field, ydst in ((g0, ydst0), (g1, ydst1), (g2, ydst2), (q0, ydstq)):
        clear_faces(field, ydst)

    def first_chunk(c):
        load(0, c).wait()
        load(1, c).wait()

        res_parts, coef_parts = [], []
        for k in range(chunk // 2):
            pair = (c * chunk + 2 * k, c * chunk + 2 * k + 1)
            for h in range(ny // 16):
                rows = slice(h * 16, h * 16 + 16)
                res_sum = coef_sum = 0.0
                for i in pair:
                    res, coef = rs[i, rows, :], dg[i, rows, :]
                    inverse = inverse_of(6.0 + coef)
                    guess = inverse * res
                    inv0[i, rows, :] = inverse
                    g0[i + 1, rows, :] = guess
                    if h == 0:
                        ysrc0[0, i] = guess[:1]
                    if h == ny // 16 - 1:
                        ysrc0[1, i] = guess[15:]
                    res_sum, coef_sum = res_sum + res, coef_sum + coef
                res_parts.append(split(res_sum))
                coef_parts.append(split(coef_sum))
        thin = joined_dot(res_parts + coef_parts, down0[...])
        for k in range(chunk // 2):
            for part in range(2):
                first = (part * (chunk // 2) + k) * ny
                for b in range(nz1 // 128):
                    pair1[part, b, c * (chunk // 2) + k] = thin[first:first + ny, b * 128:(b + 1) * 128]

    def first_step(c, carry):
        first_chunk(c)
        start_piece(0, ysrc0, ydst0, c)
        return carry

    first_chunk(0)
    pl.semaphore_wait(barrier, n_all - 1)
    start_piece(0, ysrc0, ydst0, 0)
    lax.fori_loop(1, n_chunks, first_step, 0)
    copies0 = faces(0, g0, ysrc0, ydst0, 2)
    start_faces(copies0)

    group = min(16, nx1)

    def mid_group(h, carry):
        def halved(part, i):
            return jnp.concatenate([
                pair1[part, b, i, pl.ds(0, ny1, 2), :] + pair1[part, b, i, pl.ds(1, ny1, 2), :]
                for b in range(nz1 // 128)
            ], axis=1)

        stacked = []
        for k in range(group // 2):
            planes = []
            for i in (h * group + 2 * k, h * group + 2 * k + 1):
                res, coef = halved(0, i), halved(1, i)
                inverse = inverse_of(1.5 + coef)
                guess = inverse * res
                inv1[i] = inverse * 0.25
                g1[i + 1] = guess
                ysrc1[0, i] = guess[:1]
                ysrc1[1, i] = guess[ny1 - 1:]
                planes.append((res, coef))
            stacked += [planes[0][0] + planes[1][0], planes[0][1] + planes[1][1]]
        thin = split_dot(jnp.concatenate(stacked, axis=0), down1[...])
        for k in range(group // 2):
            for part in range(2):
                first = (2 * k + part) * ny1
                pair2[part, h * (group // 2) + k] = thin[first:first + ny1]
        return carry

    lax.fori_loop(0, nx1 // group, mid_group, 0)
    copies1 = faces(1, g1, ysrc1, ydst1)
    start_faces(copies1)

    low = []
    for i in range(nx2):
        res, coef = (
            pair2[part, i, pl.ds(0, ny2, 2), :] + pair2[part, i, pl.ds(1, ny2, 2), :]
            for part in range(2))
        inverse = inverse_of(0.375 + coef)
        guess = inverse * res
        inv2[i] = inverse * 0.0625
        g2[i + 1] = guess
        ysrc2[0, i] = guess[:1]
        ysrc2[1, i] = guess[ny2 - 1:]
        low.append((res, coef))
    stacked = [
        jnp.concatenate([low[2 * k][part] + low[2 * k + 1][part] for part in range(2)], axis=1)
        for k in range(nx3)]
    pair3[...] = split_dot(jnp.concatenate(stacked, axis=0), down1[...])
    for y in range(ny3):
        gathered[core, place, y] = (
            pair3[pl.ds(2 * y, nx3, ny2), :] + pair3[pl.ds(2 * y + 1, nx3, ny2), :])

    def line_copy(k, slot):
        target = lax.rem(place + k, n_same)
        return pltpu.make_async_remote_copy(
            src_ref=gathered.at[core, slot], dst_ref=gathered.at[core, slot],
            send_sem=line_send.at[k], recv_sem=line_recv.at[slot],
            device_id=(target // n_gy * 2 + core, target % n_gy), device_id_type=MESH,
        )

    def line_start(k, carry):
        line_copy(k, place).start()
        return carry

    def line_wait(k, carry):
        line_copy(k, lax.rem(place + k, n_same)).wait_recv()
        return carry

    def twin_copy(slot):
        return pltpu.make_async_remote_copy(
            src_ref=gathered.at[slot], dst_ref=gathered.at[slot],
            send_sem=twin_send.at[0], recv_sem=twin_recv.at[0],
            device_id=(ax + 1 - 2 * core, ay), device_id_type=MESH,
        )

    lax.fori_loop(1, n_same, line_start, 0)
    copies2 = faces(2, g2, ysrc2, ydst2)
    start_faces(copies2)

    wait_faces(0, g0, ysrc0, ydst0, 2)

    def fine_smooth(c, carry):
        await_piece(0, ysrc0, ydst0, c)
        for k in range(chunk):
            i = c * chunk + k
            for r in range(ny // 8):
                q0[i + 1, band(r), :] = smooth_band(g0, inv0, ydst0, i, r)
        return carry

    lax.fori_loop(0, n_chunks, fine_smooth, 0)

    wait_faces(2, g2, ysrc2, ydst2)
    for i in range(nx2):
        smooth = jnp.concatenate([smooth_band(g2, inv2, ydst2, i, r) for r in range(ny2 // 8)], axis=0)
        dup2[i, pl.ds(0, ny2, 2), :] = smooth
        dup2[i, pl.ds(1, ny2, 2), :] = smooth

    wait_faces(1, g1, ysrc1, ydst1)

    def mid_smooth(h, carry):
        source = dup2[pl.ds(h * (group // 2), group // 2)]
        wide = split_dot(source.reshape(group // 2 * ny1, nz2), up1[...])
        for k in range(group):
            i = h * group + k
            smooth = jnp.concatenate(
                [smooth_band(g1, inv1, ydst1, i, r) for r in range(ny1 // 8)], axis=0)
            smooth += wide[k // 2 * ny1:(k // 2 + 1) * ny1]
            for b in range(nz1 // 128):
                part = smooth[:, b * 128:(b + 1) * 128]
                dup1[b, i, pl.ds(0, ny1, 2), :] = part
                dup1[b, i, pl.ds(1, ny1, 2), :] = part
        return carry

    lax.fori_loop(0, nx1 // group, mid_smooth, 0)

    lax.fori_loop(1, n_same, line_wait, 0)
    twin_copy(core).start()

    step_chunks = 2 if n_chunks % 2 == 0 else 1
    step = step_chunks * chunk

    def carry_up(c, carry):
        span = pl.ds(c * (step // 2), step // 2)
        source = jnp.concatenate(
            [dup1[b, span].reshape(step // 2 * ny, 128) for b in range(nz1 // 128)], axis=1)
        wide = split_dot(source, up0[...])
        for k in range(step):
            i = c * step + k
            smooth = q0[i + 1] + wide[k // 2 * ny:(k // 2 + 1) * ny]
            q0[i + 1] = smooth
            ysrcq[0, i] = smooth[:1]
            ysrcq[1, i] = smooth[ny - 1:]
        for k in range(step_chunks):
            start_piece(1, ysrcq, ydstq, c * step_chunks + k)
        return carry

    lax.fori_loop(0, n_chunks // step_chunks, carry_up, 0)
    copiesq = faces(3, q0, ysrcq, ydstq, 2)
    start_faces(copiesq)

    twin_copy(1 - core).wait_recv()

    wx3, wy3 = nx3 * n_gx, ny3 * n_gy
    hy3 = wy3 // 2
    lanes = 2 * nz3

    def whole(first):
        return jnp.concatenate([
            gathered[a % 2, a // 2 * n_gy + first:a // 2 * n_gy + first + n_gy // 2]
            .reshape(hy3, nx3, lanes) for a in range(n_gx)
        ], axis=1)

    lower, upper = whole(0), whole(n_gy // 2)
    shape = (hy3, wx3, lanes)
    lane, row, level = iota(shape, 2), iota(shape, 1), iota(shape, 0)
    is_low = lane < nz3
    res3 = jnp.where(is_low, lower, pltpu.roll(upper, nz3, 2))
    coef3 = jnp.where(is_low, pltpu.roll(lower, nz3, 2), upper)
    scale3 = 0.25**3
    inverse3 = relax_weight / (6.0 * scale3 + coef3)
    step3 = inverse3 * scale3
    guess3 = inverse3 * res3
    depth = jnp.where(is_low, lane, lane - nz3)
    step_ref[...] = step3
    guess_ref[...] = guess3
    flat_low = iota((8, lanes), 1) < nz3

    def one(flag):
        return jnp.where(flag, 1.0, 0.0)

    ends = one(depth == 0) + one(depth == nz3 - 1) + one(row == 0) + one(row == wx3 - 1)
    ends += one(jnp.logical_and(level == 0, is_low))
    ends += one(jnp.logical_and(level == hy3 - 1, jnp.logical_not(is_low)))
    ones_image = scale3 * ends + coef3
    ones_ref[...] = ones_image
    ones_total, res_total = jnp.sum(ones_image), jnp.sum(res3)
    old = guess_ref
    for sweep_index in range(coarse_sweeps - 1):
        new = jac_ref.at[sweep_index % 2]
        for y in range(hy3):
            for r in range(wx3 // 8):
                centre, total = band_neighbours(old.at[y], r, None, None, nz3)
                if y:
                    total += old[y - 1, band(r), :]
                else:
                    total += jnp.where(flat_low, 0.0, pltpu.roll(old[hy3 - 1, band(r), :], nz3, 1))
                if y < hy3 - 1:
                    total += old[y + 1, band(r), :]
                else:
                    total += jnp.where(flat_low, pltpu.roll(old[0, band(r), :], nz3, 1), 0.0)
                new[y, band(r), :] = (
                    (1.0 - relax_weight) * centre + guess_ref[y, band(r), :]
                    + step_ref[y, band(r), :] * total)
        old = new
    jac = old[...]
    shift = (res_total - jnp.sum(ones_ref[...] * jac)) / ones_total
    jac = jac + shift

    sol[1:hy3 + 1, nx3:nx3 + wx3, :] = jnp.where(is_low, jac, 0.0)
    sol[hy3 + 1:wy3 + 1, nx3:nx3 + wx3, :] = jnp.where(is_low, pltpu.roll(jac, nz3, 2), 0.0)

    near = sol[pl.ds(ay * ny3, ny3 + 2), pl.ds(pl.multiple_of(ax * nx3, nx3), 3 * nx3), :]
    wide = split_dot(near.reshape((ny3 + 2) * 3 * nx3, lanes), up3[...])
    expanded[...] = wide.reshape(ny3 + 2, 3 * nx3, nz)
    for y in range(ny3):
        around = expanded[y + 1]
        own = around[nx3:2 * nx3]
        column = iota(own.shape, 1)
        bands[0, y] = own
        bands[1, y] = (
            2.0 * own
            - jnp.where(column == 0, 0.0, pltpu.roll(own, 1, 1))
            - jnp.where(column == nz - 1, 0.0, pltpu.roll(own, nz - 1, 1)))
        bands[2, y] = own - expanded[y, nx3:2 * nx3]
        bands[3, y] = own - expanded[y + 2, nx3:2 * nx3]
        bands[4, y] = own - pltpu.roll(around, 1, 0)[nx3:2 * nx3]
        bands[5, y] = own - pltpu.roll(around, 3 * nx3 - 1, 0)[nx3:2 * nx3]

    wait_faces(3, q0, ysrcq, ydstq, 2)

    fold = ny // ny3

    def last_chunk(c, carry):
        await_piece(1, ysrcq, ydstq, c)

        def rows(kind):
            return [
                jnp.broadcast_to(bands[kind, y, pl.ds(c, 1), :], (fold, nz)) for y in range(ny3)]

        sub = iota((fold, nz), 0)
        rz, zq = carry
        kinds = [rows(kind) for kind in range(6)]
        for r in range(ny // 8):
            own, flat, down, up, back, ahead = (kind[r] for kind in kinds)
            edge = flat + jnp.where(sub == 0, down, 0.0) + jnp.where(sub == fold - 1, up, 0.0)
            for k in range(chunk):
                i = c * chunk + k
                centre, near_sum = band_neighbours(q0.at[i + 1], r, ydstq[0, i], ydstq[1, i])
                near_sum += q0[i, band(r), :] + q0[i + 2, band(r), :]
                precond = centre + own
                image = 6.0 * centre - near_sum + dg[i, band(r), :] * precond + edge
                if k == 0:
                    image += back
                if k == chunk - 1:
                    image += ahead
                p0[i, band(r), :] = precond
                im0[i, band(r), :] = image
                rz += rs[i, band(r), :] * precond
                zq += precond * image
        return rz, zq

    zero = jnp.zeros((fold, nz), f32)
    rz, zq = lax.fori_loop(0, n_chunks, last_chunk, (zero, zero))

    def folded(value):
        line = value.sum(axis=0, keepdims=True)
        return sum(line[:, b * 128:(b + 1) * 128] for b in range(nz // 128))

    def sum_copy(k, slot):
        return pltpu.make_async_remote_copy(
            src_ref=sums.at[slot], dst_ref=sums.at[slot],
            send_sem=sum_send.at[k], recv_sem=sum_recv.at[slot],
            device_id=other(k), device_id_type=MESH,
        )

    def sum_start(k, carry):
        sum_copy(k, me).start()
        return carry

    def sum_wait(k, carry):
        sum_copy(k, lax.rem(me + k, n_all)).wait_recv()
        return carry

    sums[me] = jnp.concatenate(
        [folded(rz), folded(zq)], axis=0)
    lax.fori_loop(1, n_all, sum_start, 0)
    lax.fori_loop(1, n_all, sum_wait, 0)
    total = sum(sums[k] for k in range(n_all))
    both = jnp.sum(total, axis=1, keepdims=True)
    alpha_ref[...] = jnp.broadcast_to(both[:1] / both[1:], alpha_ref.shape)

    for copies in (copies0, copies1, copies2, copiesq):
        for there, copy in copies:
            pl.when(there)(copy.wait_send)

    def pieces_sent(c, carry):
        for group, (ysrc, ydst) in enumerate(((ysrc0, ydst0), (ysrcq, ydstq))):
            for side in range(2):
                there, copy = piece(group, ysrc, ydst, c, side)
                pl.when(there)(copy.wait_send)
        return carry

    lax.fori_loop(0, n_chunks, pieces_sent, 0)

    def line_sent(k, carry):
        line_copy(k, place).wait_send()
        return carry

    def sum_sent(k, carry):
        sum_copy(k, me).wait_send()
        return carry

    lax.fori_loop(1, n_same, line_sent, 0)
    twin_copy(core).wait_send()
    lax.fori_loop(1, n_all, sum_sent, 0)


def scale_kernel(nx, precond, image, right, alpha_ref, update_hbm, residual_hbm, update, residual, sem):
    chunk = 8

    def store(part, c):
        source, target = ((update, update_hbm), (residual, residual_hbm))[part]
        span = pl.ds(c * chunk, chunk)
        return pltpu.make_async_copy(source.at[span], target.at[span], sem.at[part, c])

    alpha = alpha_ref[:1, :1]

    def step(c, carry):
        for k in range(chunk):
            update[c * chunk + k] = alpha * precond[c * chunk + k]
        store(0, c).start()
        for k in range(chunk):
            i = c * chunk + k
            residual[i] = right[i] - alpha * image[i]
        store(1, c).start()
        return carry

    lax.fori_loop(0, nx // chunk, step, 0)

    def finish(c, carry):
        store(0, c).wait()
        store(1, c).wait()
        return carry

    lax.fori_loop(0, nx // chunk, finish, 0)


def body(right_side, diagonal):
    n_gx, n_gy = lax.axis_size("gx"), lax.axis_size("gy")
    nx, ny, nz = right_side.shape
    V = lambda *shape: pltpu.VMEM(shape, f32)
    B = lambda *shape: pltpu.VMEM(shape, jnp.bfloat16)
    D = lambda *shape: pltpu.SemaphoreType.DMA(shape)
    nx1, ny1, nz1 = nx // 2, ny // 2, nz // 2
    nx2, ny2, nz2 = nx // 4, ny // 4, nz // 4
    nx3, ny3, nz3 = nx // 8, ny // 8, nz // 8
    block = V(nx, ny, nz)
    coarse = V(ny3 * n_gy // 2, nx3 * n_gx, 2 * nz3)
    scratch = [
        block, block, V(nx + 2, ny, nz), V(nx + 2, ny, nz),
        V(2, nx, 1, nz), V(2, nx, 1, nz), V(2, nx, 1, nz), V(2, nx, 1, nz),
        V(2, nz1 // 128, nx1, ny, 128), V(nx1, ny1, nz1), V(nx1 + 2, ny1, nz1),
        V(2, nx1, 1, nz1), V(2, nx1, 1, nz1), V(nz1 // 128, nx1, ny, 128),
        V(2, nx2, ny1, nz2), V(nx2, ny2, nz2), V(nx2 + 2, ny2, nz2),
        V(2, nx2, 1, nz2), V(2, nx2, 1, nz2), V(nx2, ny1, nz2),
        V(nx3 * ny2, 2 * nz3), V(2, n_gx // 2 * n_gy, ny3, nx3, 2 * nz3),
        V(ny3 * n_gy + 2, nx3 * (n_gx + 2), 2 * nz3), V(6, ny3, nx3, nz), V(ny3 + 2, 3 * nx3, nz),
        V(n_gx * n_gy, 2, 128), coarse, coarse, coarse, V(2, *coarse.shape),
        B(nz, nz1), B(nz1, nz2),
        B(nz1, nz), B(nz2, nz1), B(2 * nz3, nz),
        D(2, nx // 8), D(4, 4), D(4, 4), D(2, 2, nx // 8), D(2, 2, nx // 8),
        D(n_gx * n_gy), D(n_gx * n_gy), D(1), D(1), D(n_gx * n_gy), D(n_gx * n_gy),
    ]
    precond, image, right, alpha = pl.pallas_call(
        functools.partial(kernel, n_gx, n_gy, nx, ny, nz),
        out_shape=(block, block, block, V(8, 128)),
        in_specs=[pl.BlockSpec(memory_space=pl.ANY)] * 2,
        out_specs=[pl.BlockSpec(memory_space=pltpu.VMEM)] * 4,
        scratch_shapes=scratch,
        compiler_params=pltpu.CompilerParams(
            collective_id=0, has_side_effects=True, vmem_limit_bytes=40 * 1024 * 1024),
        name="cycle",
    )(right_side, diagonal)
    whole = jax.ShapeDtypeStruct(right_side.shape, f32)
    return pl.pallas_call(
        functools.partial(scale_kernel, nx),
        out_shape=(whole, whole),
        in_specs=[pl.BlockSpec(memory_space=pltpu.VMEM)] * 4,
        out_specs=[pl.BlockSpec(memory_space=pl.ANY)] * 2,
        scratch_shapes=[block, block, D(2, nx // 8)],
        compiler_params=pltpu.CompilerParams(vmem_limit_bytes=24 * 1024 * 1024),
        name="scale",
    )(precond, image, right, alpha)


def solution(mesh):
    placed = (P("gx", "gy", None), P("gx", "gy", None))
    return jax.shard_map(
        body,
        mesh=mesh,
        in_specs=placed,
        out_specs=(P("gx", "gy", None), P("gx", "gy", None)),
        check_vma=False,
    )
```

```python
import functools

import jax
import jax.numpy as jnp
from jax import lax
from jax.experimental import pallas as pl
from jax.experimental.pallas import tpu as pltpu
from jax.sharding import PartitionSpec as P

relax_weight = 0.8
coarse_sweeps = 8
MESH = pl.DeviceIdType.MESH
f32 = jnp.float32


def iota(shape, dim):
    return lax.broadcasted_iota(jnp.int32, shape, dim)


def inverse_of(value):
    guess = pl.reciprocal(value, approx=True)
    return guess * (2.0 * relax_weight - relax_weight * value * guess)


def split(value):
    high = value.astype(jnp.bfloat16)
    return high, (value - high.astype(f32)).astype(jnp.bfloat16)


def joined_dot(parts, table):
    rows = sum(high.shape[0] for high, _ in parts)
    stacked = [high for high, _ in parts] + [low for _, low in parts]
    both = jnp.dot(jnp.concatenate(stacked, axis=0), table, preferred_element_type=f32)
    return both[:rows] + both[rows:]


def split_dot(value, table):
    return joined_dot([split(value)], table)


def band(r):
    return slice(r * 8, r * 8 + 8)


def band_neighbours(plane, r, below, above, seam=0):
    rows, lanes = plane.shape
    sub, lane = iota((8, 128), 0), iota((8, 128), 1)
    first, last = lane == 0, lane == 127
    if seam:
        first = jnp.logical_or(first, lane == seam)
        last = jnp.logical_or(last, lane == seam - 1)
    centre = plane[band(r), :]
    low = plane[band(r - 1), :] if r else below
    high = plane[band(r + 1), :] if r < rows // 8 - 1 else above
    n_lanes = lanes // 128
    tiles = [centre[:, b * 128:b * 128 + 128] for b in range(n_lanes)]
    line = []
    for b, tile in enumerate(tiles):
        edge = slice(b * 128, b * 128 + 128)
        left = tiles[b - 1] if b else 0.0
        right = tiles[b + 1] if b < n_lanes - 1 else 0.0
        if seam:
            across = jnp.where(first, 0.0, pltpu.roll(tile, 1, 1))
            across += jnp.where(last, 0.0, pltpu.roll(tile, 127, 1))
        else:
            across = pltpu.roll(jnp.where(last, left, tile), 1, 1)
            across += pltpu.roll(jnp.where(first, right, tile), 127, 1)
        along = pltpu.roll(jnp.where(sub == 7, 0.0 if low is None else low[:, edge], tile), 1, 0)
        along += pltpu.roll(jnp.where(sub == 0, 0.0 if high is None else high[:, edge], tile), 7, 0)
        line.append(across + along)
    return centre, jnp.concatenate(line, axis=1) if n_lanes > 1 else line[0]


def smooth_band(field, inverse, ydst, i, r):
    centre, total = band_neighbours(field.at[i + 1], r, ydst[0, i], ydst[1, i])
    total += field[i, band(r), :] + field[i + 2, band(r), :]
    return (2.0 - relax_weight) * centre + inverse[i, band(r), :] * total


def kernel(
    n_gx, n_gy, nx, ny, nz,
    rs_hbm, dg_hbm, p0, im0, rs, alpha_ref,
    dg, inv0, g0, q0, ysrc0, ydst0, ysrcq, ydstq, ysrcw, ydstw, wide_rows,
    pair1, inv1, g1, ysrc1, ydst1, dup1,
    pair2, inv2, g2, ysrc2, ydst2, dup2,
    pair3, gathered, sol, bands, expanded, sums, step_ref, guess_ref, ones_ref, jac_ref,
    down0, down1, up0, up1, up3,
    load_sem, face_send, face_recv,
    piece_send, piece_recv, line_send, line_recv, twin_send, twin_recv, sum_send, sum_recv,
):
    ax, ay = lax.axis_index("gx"), lax.axis_index("gy")
    chunk = 8
    n_chunks = nx // chunk
    nx1, ny1, nz1 = nx // 2, ny // 2, nz // 2
    nx2, ny2, nz2 = nx // 4, ny // 4, nz // 4
    nx3, ny3, nz3 = nx // 8, ny // 8, nz // 8
    n_all = n_gx * n_gy
    n_same = n_all // 2
    core, me = ax % 2, ax * n_gy + ay
    place = ax // 2 * n_gy + ay

    def load(part, c):
        source, target = ((rs_hbm, rs), (dg_hbm, dg))[part]
        span = pl.ds(c * chunk, chunk)
        return pltpu.make_async_copy(source.at[span], target.at[span], load_sem.at[part, c])

    for c in range(n_chunks):
        load(0, c).start()
        load(1, c).start()

    barrier = pltpu.get_barrier_semaphore()

    def other(k):
        device = lax.rem(me + k, n_all)
        return (device // n_gy, device % n_gy)

    def greet(k, carry):
        pl.semaphore_signal(barrier, inc=1, device_id=other(k), device_id_type=MESH)
        return carry

    lax.fori_loop(1, n_all, greet, 0)

    def down_table(ref):
        row, column = iota(ref.shape, 0), iota(ref.shape, 1)
        ref[...] = jnp.where((row >> 1) == column, 0.125, 0.0).astype(jnp.bfloat16)

    def up_table(ref, shift):
        row, column = iota(ref.shape, 0), iota(ref.shape, 1)
        ref[...] = jnp.where(row == (column >> shift), 1.0, 0.0).astype(jnp.bfloat16)

    down_table(down0)
    down_table(down1)
    up_table(up0, 1)
    up_table(up1, 1)
    up_table(up3, 3)
    sol[...] = jnp.zeros(sol.shape, f32)

    sides = (
        (ax > 0, (ax - 1, ay)),
        (ax < n_gx - 1, (ax + 1, ay)),
        (ay > 0, (ax, ay - 1)),
        (ay < n_gy - 1, (ax, ay + 1)),
    )

    def faces(group, field, ysrc, ydst, n_sides=4):
        count = ysrc.shape[1]
        pairs = (
            (field.at[1], field.at[count + 1]),
            (field.at[count], field.at[0]),
            (ysrc.at[0], ydst.at[1]),
            (ysrc.at[1], ydst.at[0]),
        )
        copies = []
        for side, (source, target) in enumerate(pairs[:n_sides]):
            there, device = sides[side]
            copies.append((there, pltpu.make_async_remote_copy(
                src_ref=source, dst_ref=target,
                send_sem=face_send.at[group, side], recv_sem=face_recv.at[group, side ^ 1],
                device_id=device, device_id_type=MESH,
            )))
        return copies

    def start_faces(copies):
        for there, copy in copies:
            pl.when(there)(copy.start)

    def clear_faces(field, ydst):
        targets = (field.at[0], field.at[field.shape[0] - 1], ydst.at[0], ydst.at[1])
        for (there, _), target in zip(sides, targets):
            @pl.when(jnp.logical_not(there))
            def _():
                target[...] = jnp.zeros(target.shape, f32)

    def wait_faces(group, field, ysrc, ydst, n_sides=4):
        count = ysrc.shape[1]
        targets = (field.at[0], field.at[count + 1], ydst.at[0], ydst.at[1])
        for side, target in enumerate(targets[:n_sides]):
            there, device = sides[side]
            copy = pltpu.make_async_remote_copy(
                src_ref=target, dst_ref=target,
                send_sem=face_send.at[group, side], recv_sem=face_recv.at[group, side],
                device_id=device, device_id_type=MESH,
            )
            pl.when(there)(copy.wait_recv)

    def piece(group, ysrc, ydst, c, side):
        span = pl.ds(c * chunk, chunk)
        there, device = sides[2 + side]
        return there, pltpu.make_async_remote_copy(
            src_ref=ysrc.at[side, span], dst_ref=ydst.at[1 - side, span],
            send_sem=piece_send.at[group, side, c], recv_sem=piece_recv.at[group, 1 - side, c],
            device_id=device, device_id_type=MESH,
        )

    def start_piece(group, ysrc, ydst, c):
        for side in range(2):
            there, copy = piece(group, ysrc, ydst, c, side)
            pl.when(there)(copy.start)

    def await_piece(group, ysrc, ydst, c):
        for side in range(2):
            span = pl.ds(c * chunk, chunk)
            there, device = sides[2 + side]
            copy = pltpu.make_async_remote_copy(
                src_ref=ysrc.at[side, span], dst_ref=ydst.at[side, span],
                send_sem=piece_send.at[group, side, c], recv_sem=piece_recv.at[group, side, c],
                device_id=device, device_id_type=MESH,
            )
            pl.when(there)(copy.wait_recv)

    for field, ydst in ((g0, ydst0), (g1, ydst1), (g2, ydst2), (q0, ydstq), (q0, ydstw)):
        clear_faces(field, ydst)

    def first_chunk(c):
        load(0, c).wait()
        load(1, c).wait()

        res_parts, coef_parts = [], []
        for k in range(chunk // 2):
            pair = (c * chunk + 2 * k, c * chunk + 2 * k + 1)
            for h in range(ny // 16):
                rows = slice(h * 16, h * 16 + 16)
                res_sum = coef_sum = 0.0
                for i in pair:
                    res, coef = rs[i, rows, :], dg[i, rows, :]
                    inverse = inverse_of(6.0 + coef)
                    guess = inverse * res
                    inv0[i, rows, :] = inverse
                    g0[i + 1, rows, :] = guess
                    if h == 0:
                        ysrc0[0, i] = guess[:1]
                    if h == ny // 16 - 1:
                        ysrc0[1, i] = guess[15:]
                    res_sum, coef_sum = res_sum + res, coef_sum + coef
                res_parts.append(split(res_sum))
                coef_parts.append(split(coef_sum))
        thin = joined_dot(res_parts + coef_parts, down0[...])
        for k in range(chunk // 2):
            for part in range(2):
                first = (part * (chunk // 2) + k) * ny
                for b in range(nz1 // 128):
                    pair1[part, b, c * (chunk // 2) + k] = thin[first:first + ny, b * 128:(b + 1) * 128]

    def first_step(c, carry):
        first_chunk(c)
        start_piece(0, ysrc0, ydst0, c)
        return carry

    first_chunk(0)
    pl.semaphore_wait(barrier, n_all - 1)
    start_piece(0, ysrc0, ydst0, 0)
    lax.fori_loop(1, n_chunks, first_step, 0)
    copies0 = faces(0, g0, ysrc0, ydst0, 2)
    start_faces(copies0)

    group = min(16, nx1)

    def mid_group(h, carry):
        def halved(part, i):
            return jnp.concatenate([
                pair1[part, b, i, pl.ds(0, ny1, 2), :] + pair1[part, b, i, pl.ds(1, ny1, 2), :]
                for b in range(nz1 // 128)
            ], axis=1)

        stacked = []
        for k in range(group // 2):
            planes = []
            for i in (h * group + 2 * k, h * group + 2 * k + 1):
                res, coef = halved(0, i), halved(1, i)
                inverse = inverse_of(1.5 + coef)
                guess = inverse * res
                inv1[i] = inverse * 0.25
                g1[i + 1] = guess
                ysrc1[0, i] = guess[:1]
                ysrc1[1, i] = guess[ny1 - 1:]
                planes.append((res, coef))
            stacked += [planes[0][0] + planes[1][0], planes[0][1] + planes[1][1]]
        thin = split_dot(jnp.concatenate(stacked, axis=0), down1[...])
        for k in range(group // 2):
            for part in range(2):
                first = (2 * k + part) * ny1
                pair2[part, h * (group // 2) + k] = thin[first:first + ny1]
        return carry

    lax.fori_loop(0, nx1 // group, mid_group, 0)
    copies1 = faces(1, g1, ysrc1, ydst1)
    start_faces(copies1)

    low = []
    for i in range(nx2):
        res, coef = (
            pair2[part, i, pl.ds(0, ny2, 2), :] + pair2[part, i, pl.ds(1, ny2, 2), :]
            for part in range(2))
        inverse = inverse_of(0.375 + coef)
        guess = inverse * res
        inv2[i] = inverse * 0.0625
        g2[i + 1] = guess
        ysrc2[0, i] = guess[:1]
        ysrc2[1, i] = guess[ny2 - 1:]
        low.append((res, coef))
    stacked = [
        jnp.concatenate([low[2 * k][part] + low[2 * k + 1][part] for part in range(2)], axis=1)
        for k in range(nx3)]
    pair3[...] = split_dot(jnp.concatenate(stacked, axis=0), down1[...])
    for y in range(ny3):
        gathered[core, place, y] = (
            pair3[pl.ds(2 * y, nx3, ny2), :] + pair3[pl.ds(2 * y + 1, nx3, ny2), :])

    def line_copy(k, slot):
        target = lax.rem(place + k, n_same)
        return pltpu.make_async_remote_copy(
            src_ref=gathered.at[core, slot], dst_ref=gathered.at[core, slot],
            send_sem=line_send.at[k], recv_sem=line_recv.at[slot],
            device_id=(target // n_gy * 2 + core, target % n_gy), device_id_type=MESH,
        )

    def line_start(k, carry):
        line_copy(k, place).start()
        return carry

    def line_wait(k, carry):
        line_copy(k, lax.rem(place + k, n_same)).wait_recv()
        return carry

    def twin_copy(slot):
        return pltpu.make_async_remote_copy(
            src_ref=gathered.at[slot], dst_ref=gathered.at[slot],
            send_sem=twin_send.at[0], recv_sem=twin_recv.at[0],
            device_id=(ax + 1 - 2 * core, ay), device_id_type=MESH,
        )

    lax.fori_loop(1, n_same, line_start, 0)
    copies2 = faces(2, g2, ysrc2, ydst2)
    start_faces(copies2)

    wait_faces(0, g0, ysrc0, ydst0, 2)

    def fine_smooth(c, carry):
        await_piece(0, ysrc0, ydst0, c)
        for k in range(chunk):
            i = c * chunk + k
            for r in range(ny // 8):
                smooth = smooth_band(g0, inv0, ydst0, i, r)
                q0[i + 1, band(r), :] = smooth
                if r == 0:
                    ysrcq[0, i] = smooth[:1]
                if r == ny // 8 - 1:
                    ysrcq[1, i] = smooth[7:]
        start_piece(1, ysrcq, ydstq, c)
        return carry

    lax.fori_loop(0, n_chunks, fine_smooth, 0)

    wait_faces(2, g2, ysrc2, ydst2)
    for i in range(nx2):
        smooth = jnp.concatenate([smooth_band(g2, inv2, ydst2, i, r) for r in range(ny2 // 8)], axis=0)
        dup2[i, pl.ds(0, ny2, 2), :] = smooth
        dup2[i, pl.ds(1, ny2, 2), :] = smooth

    wait_faces(1, g1, ysrc1, ydst1)

    def mid_smooth(h, carry):
        source = dup2[pl.ds(h * (group // 2), group // 2)]
        wide = split_dot(source.reshape(group // 2 * ny1, nz2), up1[...])
        for k in range(group):
            i = h * group + k
            smooth = jnp.concatenate(
                [smooth_band(g1, inv1, ydst1, i, r) for r in range(ny1 // 8)], axis=0)
            smooth += wide[k // 2 * ny1:(k // 2 + 1) * ny1]
            ysrcw[0, i] = smooth[:1]
            ysrcw[1, i] = smooth[ny1 - 1:]
            for b in range(nz1 // 128):
                part = smooth[:, b * 128:(b + 1) * 128]
                dup1[b, i, pl.ds(0, ny1, 2), :] = part
                dup1[b, i, pl.ds(1, ny1, 2), :] = part
        return carry

    lax.fori_loop(0, nx1 // group, mid_smooth, 0)
    copiesw = faces(3, g1, ysrcw, ydstw)[2:]
    start_faces(copiesw)

    lax.fori_loop(1, n_same, line_wait, 0)
    twin_copy(core).start()

    step_chunks = 2 if n_chunks % 2 == 0 else 1
    step = step_chunks * chunk

    def carry_up(c, carry):
        span = pl.ds(c * (step // 2), step // 2)
        source = jnp.concatenate(
            [dup1[b, span].reshape(step // 2 * ny, 128) for b in range(nz1 // 128)], axis=1)
        wide = split_dot(source, up0[...])
        for k in range(step):
            i = c * step + k
            q0[i + 1] = q0[i + 1] + wide[k // 2 * ny:(k // 2 + 1) * ny]
        return carry

    lax.fori_loop(0, n_chunks // step_chunks, carry_up, 0)
    copiesq = faces(3, q0, ysrcq, ydstq, 2)
    start_faces(copiesq)

    twin_copy(1 - core).wait_recv()

    wx3, wy3 = nx3 * n_gx, ny3 * n_gy
    hy3 = wy3 // 2
    lanes = 2 * nz3

    def whole(first):
        return jnp.concatenate([
            gathered[a % 2, a // 2 * n_gy + first:a // 2 * n_gy + first + n_gy // 2]
            .reshape(hy3, nx3, lanes) for a in range(n_gx)
        ], axis=1)

    lower, upper = whole(0), whole(n_gy // 2)
    shape = (hy3, wx3, lanes)
    lane, row, level = iota(shape, 2), iota(shape, 1), iota(shape, 0)
    is_low = lane < nz3
    res3 = jnp.where(is_low, lower, pltpu.roll(upper, nz3, 2))
    coef3 = jnp.where(is_low, pltpu.roll(lower, nz3, 2), upper)
    scale3 = 0.25**3
    inverse3 = relax_weight / (6.0 * scale3 + coef3)
    step3 = inverse3 * scale3
    guess3 = inverse3 * res3
    depth = jnp.where(is_low, lane, lane - nz3)
    step_ref[...] = step3
    guess_ref[...] = guess3
    flat_low = iota((8, lanes), 1) < nz3

    def one(flag):
        return jnp.where(flag, 1.0, 0.0)

    ends = one(depth == 0) + one(depth == nz3 - 1) + one(row == 0) + one(row == wx3 - 1)
    ends += one(jnp.logical_and(level == 0, is_low))
    ends += one(jnp.logical_and(level == hy3 - 1, jnp.logical_not(is_low)))
    ones_image = scale3 * ends + coef3
    ones_ref[...] = ones_image
    ones_total, res_total = jnp.sum(ones_image), jnp.sum(res3)
    old = guess_ref
    for sweep_index in range(coarse_sweeps - 1):
        new = jac_ref.at[sweep_index % 2]
        for y in range(hy3):
            for r in range(wx3 // 8):
                centre, total = band_neighbours(old.at[y], r, None, None, nz3)
                if y:
                    total += old[y - 1, band(r), :]
                else:
                    total += jnp.where(flat_low, 0.0, pltpu.roll(old[hy3 - 1, band(r), :], nz3, 1))
                if y < hy3 - 1:
                    total += old[y + 1, band(r), :]
                else:
                    total += jnp.where(flat_low, pltpu.roll(old[0, band(r), :], nz3, 1), 0.0)
                new[y, band(r), :] = (
                    (1.0 - relax_weight) * centre + guess_ref[y, band(r), :]
                    + step_ref[y, band(r), :] * total)
        old = new
    jac = old[...]
    shift = (res_total - jnp.sum(ones_ref[...] * jac)) / ones_total
    jac = jac + shift

    sol[1:hy3 + 1, nx3:nx3 + wx3, :] = jnp.where(is_low, jac, 0.0)
    sol[hy3 + 1:wy3 + 1, nx3:nx3 + wx3, :] = jnp.where(is_low, pltpu.roll(jac, nz3, 2), 0.0)

    near = sol[pl.ds(ay * ny3, ny3 + 2), pl.ds(pl.multiple_of(ax * nx3, nx3), 3 * nx3), :]
    wide = split_dot(near.reshape((ny3 + 2) * 3 * nx3, lanes), up3[...])
    expanded[...] = wide.reshape(ny3 + 2, 3 * nx3, nz)
    for y in range(ny3):
        around = expanded[y + 1]
        own = around[nx3:2 * nx3]
        column = iota(own.shape, 1)
        bands[0, y] = own
        bands[1, y] = (
            2.0 * own
            - jnp.where(column == 0, 0.0, pltpu.roll(own, 1, 1))
            - jnp.where(column == nz - 1, 0.0, pltpu.roll(own, nz - 1, 1)))
        bands[2, y] = own - expanded[y, nx3:2 * nx3]
        bands[3, y] = own - expanded[y + 2, nx3:2 * nx3]
        bands[4, y] = own - pltpu.roll(around, 1, 0)[nx3:2 * nx3]
        bands[5, y] = own - pltpu.roll(around, 3 * nx3 - 1, 0)[nx3:2 * nx3]

    wait_faces(3, q0, ysrcq, ydstq, 2)
    for side in range(2):
        there, device = sides[2 + side]
        copy = pltpu.make_async_remote_copy(
            src_ref=ysrcw.at[side], dst_ref=ydstw.at[side],
            send_sem=face_send.at[3, 2 + side], recv_sem=face_recv.at[3, 2 + side],
            device_id=device, device_id_type=MESH,
        )
        pl.when(there)(copy.wait_recv)
    for side in range(2):
        wide = split_dot(jnp.concatenate([ydstw[side, j] for j in range(nx1)], axis=0), up0[...])
        for j in range(nx1):
            wide_rows[side, j] = wide[j:j + 1]

    fold = ny // ny3

    def last_chunk(c, carry):
        await_piece(1, ysrcq, ydstq, c)

        def rows(kind):
            return [
                jnp.broadcast_to(bands[kind, y, pl.ds(c, 1), :], (fold, nz)) for y in range(ny3)]

        sub = iota((fold, nz), 0)
        rz, zq = carry
        kinds = [rows(kind) for kind in range(6)]
        for r in range(ny // 8):
            own, flat, down, up, back, ahead = (kind[r] for kind in kinds)
            edge = flat + jnp.where(sub == 0, down, 0.0) + jnp.where(sub == fold - 1, up, 0.0)
            for k in range(chunk):
                i = c * chunk + k
                centre, near_sum = band_neighbours(
                    q0.at[i + 1], r,
                    ydstq[0, i] + wide_rows[0, i // 2] if r == 0 else None,
                    ydstq[1, i] + wide_rows[1, i // 2] if r == ny // 8 - 1 else None)
                near_sum += q0[i, band(r), :] + q0[i + 2, band(r), :]
                precond = centre + own
                image = 6.0 * centre - near_sum + dg[i, band(r), :] * precond + edge
                if k == 0:
                    image += back
                if k == chunk - 1:
                    image += ahead
                p0[i, band(r), :] = precond
                im0[i, band(r), :] = image
                rz += rs[i, band(r), :] * precond
                zq += precond * image
        return rz, zq

    zero = jnp.zeros((fold, nz), f32)
    rz, zq = lax.fori_loop(0, n_chunks, last_chunk, (zero, zero))

    def folded(value):
        line = value.sum(axis=0, keepdims=True)
        return sum(line[:, b * 128:(b + 1) * 128] for b in range(nz // 128))

    def sum_copy(k, slot):
        return pltpu.make_async_remote_copy(
            src_ref=sums.at[slot], dst_ref=sums.at[slot],
            send_sem=sum_send.at[k], recv_sem=sum_recv.at[slot],
            device_id=other(k), device_id_type=MESH,
        )

    def sum_start(k, carry):
        sum_copy(k, me).start()
        return carry

    def sum_wait(k, carry):
        sum_copy(k, lax.rem(me + k, n_all)).wait_recv()
        return carry

    sums[me] = jnp.concatenate(
        [folded(rz), folded(zq)], axis=0)
    lax.fori_loop(1, n_all, sum_start, 0)
    lax.fori_loop(1, n_all, sum_wait, 0)
    total = sum(sums[k] for k in range(n_all))
    both = jnp.sum(total, axis=1, keepdims=True)
    alpha_ref[...] = jnp.broadcast_to(both[:1] / both[1:], alpha_ref.shape)

    for copies in (copies0, copies1, copies2, copiesq, copiesw):
        for there, copy in copies:
            pl.when(there)(copy.wait_send)

    def pieces_sent(c, carry):
        for group, (ysrc, ydst) in enumerate(((ysrc0, ydst0), (ysrcq, ydstq))):
            for side in range(2):
                there, copy = piece(group, ysrc, ydst, c, side)
                pl.when(there)(copy.wait_send)
        return carry

    lax.fori_loop(0, n_chunks, pieces_sent, 0)

    def line_sent(k, carry):
        line_copy(k, place).wait_send()
        return carry

    def sum_sent(k, carry):
        sum_copy(k, me).wait_send()
        return carry

    lax.fori_loop(1, n_same, line_sent, 0)
    twin_copy(core).wait_send()
    lax.fori_loop(1, n_all, sum_sent, 0)


def scale_kernel(nx, precond, image, right, alpha_ref, update_hbm, residual_hbm, update, residual, sem):
    chunk = 8

    def store(part, c):
        source, target = ((update, update_hbm), (residual, residual_hbm))[part]
        span = pl.ds(c * chunk, chunk)
        return pltpu.make_async_copy(source.at[span], target.at[span], sem.at[part, c])

    alpha = alpha_ref[:1, :1]

    def step(c, carry):
        for k in range(chunk):
            update[c * chunk + k] = alpha * precond[c * chunk + k]
        store(0, c).start()
        for k in range(chunk):
            i = c * chunk + k
            residual[i] = right[i] - alpha * image[i]
        store(1, c).start()
        return carry

    lax.fori_loop(0, nx // chunk, step, 0)

    def finish(c, carry):
        store(0, c).wait()
        store(1, c).wait()
        return carry

    lax.fori_loop(0, nx // chunk, finish, 0)


def body(right_side, diagonal):
    n_gx, n_gy = lax.axis_size("gx"), lax.axis_size("gy")
    nx, ny, nz = right_side.shape
    V = lambda *shape: pltpu.VMEM(shape, f32)
    B = lambda *shape: pltpu.VMEM(shape, jnp.bfloat16)
    D = lambda *shape: pltpu.SemaphoreType.DMA(shape)
    nx1, ny1, nz1 = nx // 2, ny // 2, nz // 2
    nx2, ny2, nz2 = nx // 4, ny // 4, nz // 4
    nx3, ny3, nz3 = nx // 8, ny // 8, nz // 8
    block = V(nx, ny, nz)
    coarse = V(ny3 * n_gy // 2, nx3 * n_gx, 2 * nz3)
    scratch = [
        block, block, V(nx + 2, ny, nz), V(nx + 2, ny, nz),
        V(2, nx, 1, nz), V(2, nx, 1, nz), V(2, nx, 1, nz), V(2, nx, 1, nz),
        V(2, nx1, 1, nz1), V(2, nx1, 1, nz1), V(2, nx1, 1, nz),
        V(2, nz1 // 128, nx1, ny, 128), V(nx1, ny1, nz1), V(nx1 + 2, ny1, nz1),
        V(2, nx1, 1, nz1), V(2, nx1, 1, nz1), V(nz1 // 128, nx1, ny, 128),
        V(2, nx2, ny1, nz2), V(nx2, ny2, nz2), V(nx2 + 2, ny2, nz2),
        V(2, nx2, 1, nz2), V(2, nx2, 1, nz2), V(nx2, ny1, nz2),
        V(nx3 * ny2, 2 * nz3), V(2, n_gx // 2 * n_gy, ny3, nx3, 2 * nz3),
        V(ny3 * n_gy + 2, nx3 * (n_gx + 2), 2 * nz3), V(6, ny3, nx3, nz), V(ny3 + 2, 3 * nx3, nz),
        V(n_gx * n_gy, 2, 128), coarse, coarse, coarse, V(2, *coarse.shape),
        B(nz, nz1), B(nz1, nz2),
        B(nz1, nz), B(nz2, nz1), B(2 * nz3, nz),
        D(2, nx // 8), D(4, 4), D(4, 4), D(2, 2, nx // 8), D(2, 2, nx // 8),
        D(n_gx * n_gy), D(n_gx * n_gy), D(1), D(1), D(n_gx * n_gy), D(n_gx * n_gy),
    ]
    precond, image, right, alpha = pl.pallas_call(
        functools.partial(kernel, n_gx, n_gy, nx, ny, nz),
        out_shape=(block, block, block, V(8, 128)),
        in_specs=[pl.BlockSpec(memory_space=pl.ANY)] * 2,
        out_specs=[pl.BlockSpec(memory_space=pltpu.VMEM)] * 4,
        scratch_shapes=scratch,
        compiler_params=pltpu.CompilerParams(
            collective_id=0, has_side_effects=True, vmem_limit_bytes=40 * 1024 * 1024),
        name="cycle",
    )(right_side, diagonal)
    whole = jax.ShapeDtypeStruct(right_side.shape, f32)
    return pl.pallas_call(
        functools.partial(scale_kernel, nx),
        out_shape=(whole, whole),
        in_specs=[pl.BlockSpec(memory_space=pltpu.VMEM)] * 4,
        out_specs=[pl.BlockSpec(memory_space=pl.ANY)] * 2,
        scratch_shapes=[block, block, D(2, nx // 8)],
        compiler_params=pltpu.CompilerParams(vmem_limit_bytes=24 * 1024 * 1024),
        name="scale",
    )(precond, image, right, alpha)


def solution(mesh):
    placed = (P("gx", "gy", None), P("gx", "gy", None))
    return jax.shard_map(
        body,
        mesh=mesh,
        in_specs=placed,
        out_specs=(P("gx", "gy", None), P("gx", "gy", None)),
        check_vma=False,
    )
```
